512 devices in a mesh: group: 4 (over x_lo, core), expert: 64 (over y, z), tensor: 2 (over x_hi).
Axes of the slice: x: 4 (x_hi: 2, x_lo: 2; x = x_hi * 2 + x_lo), y: 8, z: 8, core: 2. Of those that a mesh axis runs over, the one named last changes fastest.
Arguments:
- hidden_rows: bfloat16 [1024, 3584], P('expert'), may hold values from -6 to 6
- parent_beam: int32 [1024], P('expert'), may hold values from 0 to 3
- norm_gain: float32 [3584], replicated, may hold values from 0.5 to 1.5
- route_ids: int32 [1024, 8], P('expert'), may hold values from 0 to 63, all different within a row; in each aligned block of 16 rows (0 to 15, 16 to 31, ...) at most 4 rows name the same one
- route_weight: float32 [1024, 8], P('expert'), may hold values from 0.05 to 0.5
- expert_weight: bfloat16 [64, 3584, 2, 1024], P('expert', None, None, ('group', 'tensor')), may hold values from -0.09375 to 0.09375
- learn_tokens: bfloat16 [8192, 3584], P('expert'), may hold values from -6 to 6
- learn_live: int32 [8192], P('expert'), may hold values 0 or 1
- cotangent: bfloat16 [8192, 1024], P('expert', ('group', 'tensor')), may hold values from -0.52734375 to 0.52734375
- master: float32 [3584, 2, 1024], P('expert', None, ('group', 'tensor')), may hold values from -0.09375 to 0.09375
- first_moment: float32 [3584, 2, 1024], P('expert', None, ('group', 'tensor')), may hold values from -4 to 4
- second_moment: float32 [3584, 2, 1024], P('expert', None, ('group', 'tensor')), may hold values from 0.05 to 1
Outputs:
- rolled: bfloat16 [1024, 8, 1024], P('expert', None, ('group', 'tensor'))
- new_master: float32 [3584, 2, 1024], P('expert', None, ('group', 'tensor'))
- new_first: float32 [3584, 2, 1024], P('expert', None, ('group', 'tensor'))
- new_second: float32 [3584, 2, 1024], P('expert', None, ('group', 'tensor'))
- fresh: bfloat16 [3584, 2, 1024], P(None, None, ('group', 'tensor'))
The draws below stay inside these ranges and needn't reach their ends.
Inputs may be any that keep to these rules, and one draw needn't show every extreme that they name: `route_ids`: in each aligned block of 16 rows (the rows of one device) the 8 experts of a row differ, no expert is named by more than 4 rows, a bound that some block reaches. `parent_beam`: rows 4 * q to 4 * q + 3 are the beams of one request.
All inputs are finite; a program needn't handle non-finite values. No bound on the sum of `learn_live` on one device may be relied on, other than what follows from the above.
Results may differ from the reference program's by a relative error of at most 0.0065.
Values may be sent and summed in bfloat16 or wider, within the bound.
No kernel may reach another device: no remote copies, remote signals or barrier semaphores. Data moves between devices by JAX's collectives and lax.ppermute only.
A program may use at most 64 MiB of HBM per device.

```python
import math
import jax
import jax.numpy as jnp
import numpy as np
from jax import lax

D = 3584
HID = 1024
EXPERTS = 64
TOP = 8
BEAMS = 4
CAP = 4
ROWS_DEV = 16
ROWS = 1024
TOKENS_L = 8192
N_EXPERT = 64


def touch_ends(entries, own_key, least, high):
    index_at = [jax.random.randint(jax.random.fold_in(own_key, axis), (), 0, length) for axis, length in enumerate(entries.shape)]
    widest = entries.shape.index(max(entries.shape))
    beside = index_at[:widest] + [(index_at[widest] + 1) % entries.shape[widest]] + index_at[widest + 1:]
    return entries.at[tuple(index_at)].set(least).at[tuple(beside)].set(high)


def block_scale(key, extent, cuts, smallest, largest):
    factor_of, own = 1.0, jax.random.fold_in(key, 6)
    for dim, shards_of in cuts:
        draws = jnp.exp(jax.random.uniform(jax.random.fold_in(own, dim), (shards_of,), jnp.float32, smallest / len(cuts), largest / len(cuts)))
        factor_of = factor_of * jnp.repeat(draws, extent[dim] // shards_of).reshape([-1 if axis == dim else 1 for axis in range(len(extent))])
    return factor_of


def shared_out(own_key, own, number, rows, amount, top, bound, skew):
    order = jax.random.permutation(own_key, amount)
    crowded, usual = load_shares(amount, rows * top, bound, skew, True), load_shares(amount, rows * top, bound, skew, False)
    places = jnp.arange(amount)

    def named(lengths, turn):
        used = int((lengths > 0).sum())
        fixed = max(1, used // 4)
        passed = fixed + (places - fixed + turn * (used - fixed)) % max(1, amount - fixed)
        return jnp.zeros((amount,), jnp.int32).at[order[jnp.where(places < fixed, places, passed)]].set(jnp.asarray(lengths, jnp.int32))

    lengths = jnp.where(number % 4 == 0, named(crowded, number // 4), named(usual, number - number // 4 - 1))
    mixed = jax.random.permutation(jax.random.fold_in(own, 3), amount)
    source_of, receiver = mixed[0:amount // 2 * 2:2], mixed[1:amount // 2 * 2:2]
    margin = jnp.minimum(lengths[source_of] - 1, bound - lengths[receiver]) // 2
    margin = jnp.where((source_of == order[0]) | (receiver == order[0]) | (lengths[receiver] == 0), 0, jnp.maximum(margin, 0))
    passed = jax.random.randint(jax.random.fold_in(own, 4), (amount // 2,), 0, 1 << 20) % (margin + 1)
    lengths = lengths.at[source_of].add(-passed).at[receiver].add(passed)
    members = jnp.searchsorted(jnp.cumsum(lengths), jnp.arange(rows * top), side="right").astype(jnp.int32)
    listing = members.reshape(top, rows).T
    listing = listing[jax.random.permutation(jax.random.fold_in(own, 1), rows)]
    turn = jax.random.randint(jax.random.fold_in(own, 2), (rows, 1), 0, top)
    return jnp.take_along_axis(listing, (jnp.arange(top)[None, :] + turn) % top, axis=1)


def load_shares(amount, total, most, skew, full):
    portions = [(1 << 20) // math.isqrt(rank ** skew) + 1 for rank in range(1, amount + 1)]
    largest = most if full else min(most, max(-(-total // amount), total * portions[0] // sum(portions)))
    least = 1 if total - largest >= amount - 1 else 0
    holding, rest = [largest] + [least] * (amount - 1), total - largest - least * (amount - 1)
    while rest > 0:
        free = [i for i in range(1, amount) if holding[i] < largest] or [i for i in range(1, amount) if holding[i] < most]
        whole, budget = sum([portions[i] for i in free]), rest
        for i in free:
            extra = min(most - holding[i], max(1, budget * portions[i] // whole), rest)
            holding[i] = holding[i] + extra
            rest = rest - extra
    return np.array(holding)


def noise(rng, shape, scale, most, split=(), held_as=jnp.bfloat16):
    values = scale * jax.random.normal(rng, shape, jnp.float32)
    if split:
        values = values * block_scale(rng, shape, split, -0.22, 0.18)
    return jnp.clip(values, -most, most).astype(held_as)


def setup_inputs(seed: int = 0) -> dict:
    seeds = jax.random.split(jax.random.key(seed), 13)
    hidden_rows = noise(seeds[0], (ROWS, D), 1.0, 6.0, ((0, 64),))
    parent_beam = touch_ends(jax.random.randint(seeds[1], (ROWS,), 0, BEAMS), jax.random.fold_in(seeds[1], 1), 0, BEAMS - 1).astype(jnp.int32)
    norm_gain = jnp.clip(1.0 + 0.1 * jax.random.normal(seeds[2], (D,), jnp.float32), 0.5, 1.5)
    route_ids_keys = jax.random.split(jax.random.fold_in(seeds[3], 1), ROWS // ROWS_DEV)
    route_ids_turns = jax.random.permutation(jax.random.fold_in(seeds[3], 3), ROWS // ROWS_DEV)
    route_ids = jax.vmap(lambda own, number: shared_out(jax.random.fold_in(seeds[3], 2), own, number, ROWS_DEV, EXPERTS, TOP, CAP, 1))(route_ids_keys, route_ids_turns).reshape((ROWS, TOP))
    route_weight = jnp.clip(0.05 + 0.45 * jax.random.uniform(seeds[4], (ROWS, TOP), jnp.float32) ** block_scale(seeds[4], (ROWS, TOP), ((0, 64),), -0.2, 0.2), 0.05, 0.5)
    expert_weight = noise(seeds[5], (EXPERTS, D, 2, HID), D ** -0.5, 0.09375, ((0, 64), (3, 8)))
    learn_tokens = noise(seeds[6], (TOKENS_L, D), 1.0, 6.0, ((0, 64),))
    learn_live = touch_ends((jax.random.randint(seeds[7], (TOKENS_L,), 0, 4) < 3).astype(jnp.int32), jax.random.fold_in(seeds[7], 1), 0, 1)
    cotangent = noise(seeds[8], (TOKENS_L, HID), (8 * TOKENS_L ** -0.5), 0.52734375, ((0, 64), (1, 8)))
    master = noise(seeds[9], (D, 2, HID), D ** -0.5, 0.09375, ((0, 64), (2, 8)), jnp.float32)
    first_moment = noise(seeds[10], (D, 2, HID), 0.5, 4.0, ((0, 64), (2, 8)), jnp.float32)
    second_moment = jnp.clip(jnp.exp(math.log(1.0) - 2.9957323 * jax.random.uniform(seeds[11], (D, 2, HID), jnp.float32) ** block_scale(seeds[11], (D, 2, HID), ((0, 64), (2, 8)), -0.2, 0.2)), 0.05, 1.0)
    return dict(hidden_rows=hidden_rows, parent_beam=parent_beam, norm_gain=norm_gain, route_ids=route_ids, route_weight=route_weight, expert_weight=expert_weight, learn_tokens=learn_tokens, learn_live=learn_live, cotangent=cotangent, master=master, first_moment=first_moment, second_moment=second_moment)


def reference(hidden_rows, parent_beam, norm_gain, route_ids, route_weight, expert_weight, learn_tokens, learn_live, cotangent, master, first_moment, second_moment):
    total_rows = hidden_rows.shape[0]
    grouped = hidden_rows.reshape(total_rows // BEAMS, BEAMS, D)
    picks = jnp.broadcast_to(parent_beam.reshape(total_rows // BEAMS, BEAMS, 1), (total_rows // BEAMS, BEAMS, D)).astype(jnp.int32)
    reordered = jnp.take_along_axis(grouped, picks, axis=1).reshape(total_rows, D).astype(jnp.float32)
    mean_square = lax.optimization_barrier(jnp.mean(reordered * reordered, axis=1, keepdims=True))
    normed = (reordered * lax.rsqrt(mean_square + 1e-06) * norm_gain[None, :]).astype(jnp.bfloat16)
    flat_ids = route_ids.reshape(-1).astype(jnp.int32)
    capacity_all = N_EXPERT * CAP

    def one_expert(carry, expert):
        elsewhere = (flat_ids != expert).astype(jnp.int32)
        chosen = jnp.argsort(elsewhere, stable=True)[:capacity_all].astype(jnp.int32)
        usable = (flat_ids[chosen] == expert).astype(jnp.float32)[:, None]
        rows_in = normed[chosen // TOP]
        expert_matrix = expert_weight[expert].reshape(D, 2 * HID)
        projected = jnp.dot(rows_in, expert_matrix, preferred_element_type=jnp.float32)
        gate_part = projected[:, :HID]
        activated = (gate_part * jax.nn.sigmoid(gate_part) * projected[:, HID:]).astype(jnp.bfloat16)
        activated = lax.optimization_barrier(activated).astype(jnp.float32) * usable
        return (carry.at[chosen].add(activated), None)
    start_carry = jnp.zeros((flat_ids.shape[0], HID), jnp.float32)
    gathered, _ = lax.scan(one_expert, start_carry, jnp.arange(EXPERTS, dtype=jnp.int32))
    rolled = (gathered * route_weight.reshape(-1, 1)).astype(jnp.bfloat16).reshape(total_rows, TOP, HID)
    weights = master.astype(jnp.bfloat16).reshape(D, 2 * HID)
    projected = jnp.dot(learn_tokens, weights, preferred_element_type=jnp.float32)
    gate_pre = projected[:, :HID]
    up_pre = projected[:, HID:]
    sigmoid_gate = jax.nn.sigmoid(gate_pre)
    upstream = cotangent.astype(jnp.float32) * learn_live.astype(jnp.float32)[:, None]
    slope = sigmoid_gate * (1.0 + gate_pre * (1.0 - sigmoid_gate))
    grad_pre = jnp.concatenate([upstream * up_pre * slope, upstream * gate_pre * sigmoid_gate], axis=1).astype(jnp.bfloat16)
    gradient = lax.dot_general(learn_tokens, grad_pre, (((0,), (0,)), ((), ())), preferred_element_type=jnp.float32).reshape(D, 2, HID)
    new_first = 0.9 * first_moment + 0.1 * gradient
    new_second = 0.95 * second_moment + 0.05 * gradient * gradient
    correct_one = 1.0 - 0.9 ** 10
    correct_two = 1.0 - 0.95 ** 10
    update = new_first / correct_one / (jnp.sqrt(new_second / correct_two) + 1e-08)
    new_master = master - 0.01 * (update + 0.1 * master)
    fresh = new_master.astype(jnp.bfloat16)
    return (rolled, new_master, new_first, new_second, fresh)
```

```python
import jax
import jax.numpy as jnp
from jax import lax
from jax.sharding import Mesh, PartitionSpec as P

EXPERTS = 64
TOP = 8
BEAMS = 4
CAP = 4

beta_one = 0.9
beta_two = 0.95
learn_rate = 0.01
decay_rate = 0.1
epsilon = 1e-08
norm_epsilon = 1e-06
adam_step = 10.0

ROW = ("y", "z")
COLUMN = ("xl", "core", "xh")
weight_scale = 2.0**19
fresh_scale = 2.0**16


def to_half(values, scale):
    return (values.astype(jnp.bfloat16).astype(jnp.float32) * scale).astype(jnp.float16)


def from_half(values, scale):
    return (values.astype(jnp.float32) * (1.0 / scale)).astype(jnp.bfloat16)


def gather_by_exchange(block, axis):
    count = lax.axis_size(axis)
    return lax.all_to_all(
        jnp.broadcast_to(block[None], (count,) + block.shape), axis, 0, 0, tiled=True
    )


def shards(
    hidden_rows,
    parent_beam,
    norm_gain,
    route_ids,
    route_weight,
    expert_weight,
    learn_tokens,
    learn_live,
    cotangent,
    master,
    first_moment,
    second_moment,
):
    hid_local = master.shape[2]
    own_rows = master.shape[0]
    wide = 2 * hid_local
    n_y, n_z = lax.axis_size("y"), lax.axis_size("z")
    n_x = lax.axis_size(COLUMN)

    token_slice = lax.all_to_all(learn_tokens, "y", split_axis=1, concat_axis=0, tiled=True)

    rows_dev, width = hidden_rows.shape
    grouped = hidden_rows.reshape(rows_dev // BEAMS, BEAMS, width)
    selector = (
        parent_beam.reshape(rows_dev // BEAMS, BEAMS, 1)
        == jnp.arange(BEAMS, dtype=jnp.int32)[None, None, :]
    ).astype(jnp.bfloat16)
    reordered = jnp.einsum(
        "rbc,rcd->rbd", selector, grouped, preferred_element_type=jnp.float32
    ).reshape(rows_dev, width)
    mean_square = jnp.mean(reordered * reordered, axis=1, keepdims=True)
    normed = (reordered * lax.rsqrt(mean_square + norm_epsilon) * norm_gain[None, :]).astype(
        jnp.bfloat16
    )
    flat_ids = route_ids.reshape(rows_dev * TOP)
    onehot = (flat_ids[:, None] == jnp.arange(EXPERTS, dtype=jnp.int32)[None, :]).astype(jnp.int32)
    earlier = jnp.cumsum(onehot, axis=0) - onehot
    position = jnp.sum(earlier * onehot, axis=1)
    slot_index = flat_ids * CAP + position
    slot_table = (
        slot_index[:, None] == jnp.arange(EXPERTS * CAP, dtype=jnp.int32)[None, :]
    ).astype(jnp.float32)
    row_table = slot_table.reshape(rows_dev, TOP, EXPERTS * CAP).sum(axis=1).astype(jnp.bfloat16)
    share = width // n_x
    normed_share = lax.dynamic_index_in_dim(
        normed.reshape(rows_dev, n_x, share), lax.axis_index(COLUMN), axis=1, keepdims=False
    )
    outgoing = lax.dot_general(
        row_table, normed_share, (((0,), (0,)), ((), ())), preferred_element_type=jnp.float32
    ).astype(jnp.bfloat16)
    arrived = lax.all_to_all(
        outgoing.reshape(n_y * n_z, CAP, share), ROW, split_axis=0, concat_axis=0, tiled=True
    )
    arrived = gather_by_exchange(arrived.reshape(EXPERTS * CAP, share), COLUMN)
    arrived = arrived.reshape(n_x, EXPERTS * CAP, share)

    weights = lax.all_gather(
        to_half(master, weight_scale).reshape(own_rows, wide), ROW, axis=0, tiled=True
    )
    projected = jnp.dot(
        learn_tokens, from_half(weights, weight_scale), preferred_element_type=jnp.float32
    )
    gate_pre = projected[:, :hid_local]
    up_pre = projected[:, hid_local:]
    sigmoid_gate = jax.nn.sigmoid(gate_pre)
    upstream = cotangent.astype(jnp.float32) * learn_live.astype(jnp.float32)[:, None]
    slope = sigmoid_gate * (1.0 + gate_pre * (1.0 - sigmoid_gate))
    grad_pre = jnp.concatenate(
        [upstream * up_pre * slope, upstream * gate_pre * sigmoid_gate], axis=1
    ).astype(jnp.bfloat16)

    grad_all = gather_by_exchange(grad_pre, "y").reshape(token_slice.shape[0], wide)
    partial = lax.dot_general(
        token_slice, grad_all, (((0,), (0,)), ((), ())), preferred_element_type=jnp.float32
    ).astype(jnp.bfloat16)
    parts = lax.all_to_all(
        partial.reshape(n_z, own_rows, wide), "z", split_axis=0, concat_axis=0, tiled=True
    )
    gradient = jnp.sum(parts.astype(jnp.float32), axis=0).reshape(master.shape)
    new_first = beta_one * first_moment + (1.0 - beta_one) * gradient
    new_second = beta_two * second_moment + (1.0 - beta_two) * gradient * gradient
    correct_one = 1.0 - beta_one**adam_step
    correct_two = 1.0 - beta_two**adam_step
    update = new_first / correct_one / (jnp.sqrt(new_second / correct_two) + epsilon)
    new_master = master - learn_rate * (update + decay_rate * master)
    fresh_rows = gather_by_exchange(to_half(new_master, fresh_scale), "z")
    fresh_rows = fresh_rows.reshape(n_z * own_rows, 2, hid_local)
    fresh = from_half(lax.all_gather(fresh_rows, "y", axis=0, tiled=True), fresh_scale)

    local_weight = expert_weight.reshape(n_x, share, wide)
    projected_rows = jnp.einsum(
        "jsd,jdk->sk", arrived, local_weight, preferred_element_type=jnp.float32
    )
    gate_rows = projected_rows[:, :hid_local]
    activated_rows = (
        gate_rows * jax.nn.sigmoid(gate_rows) * projected_rows[:, hid_local:]
    ).astype(jnp.bfloat16)
    returned = lax.all_to_all(
        activated_rows.reshape(n_y * n_z, CAP, hid_local), ROW, split_axis=0, concat_axis=0, tiled=True
    )
    back_slots = returned.reshape(EXPERTS * CAP, hid_local)
    picked = jnp.dot(
        slot_table.astype(jnp.bfloat16), back_slots, preferred_element_type=jnp.float32
    )
    rolled = (
        (picked * route_weight.reshape(rows_dev * TOP, 1))
        .astype(jnp.bfloat16)
        .reshape(rows_dev, TOP, hid_local)
    )
    return (rolled, new_master, new_first, new_second, fresh)


def solution(mesh):
    fine = Mesh(mesh.devices.reshape(2, 2, 8, 8, 2), ("xl", "core", "y", "z", "xh"))
    placed = (
        P(ROW, None),
        P(ROW),
        P(),
        P(ROW, None),
        P(ROW, None),
        P(ROW, None, None, COLUMN),
        P(ROW, None),
        P(ROW),
        P(ROW, COLUMN),
        P(ROW, None, COLUMN),
        P(ROW, None, COLUMN),
        P(ROW, None, COLUMN),
    )
    return jax.shard_map(
        shards,
        mesh=fine,
        in_specs=placed,
        out_specs=(
            P(ROW, None, COLUMN),
            P(ROW, None, COLUMN),
            P(ROW, None, COLUMN),
            P(ROW, None, COLUMN),
            P(None, None, COLUMN),
        ),
        check_vma=False,
    )
```

```python
import jax
import jax.numpy as jnp
from jax import lax
from jax.sharding import Mesh, PartitionSpec as P

EXPERTS = 64
TOP = 8
BEAMS = 4
CAP = 4

beta_one = 0.9
beta_two = 0.95
learn_rate = 0.01
decay_rate = 0.1
epsilon = 1e-08
norm_epsilon = 1e-06
adam_step = 10.0

ROW = ("y", "z")
COLUMN = ("xl", "core", "xh")
SWAP = [(0, 1), (1, 0)]
pre_scale = 2.0**7
grad_scale = 2.0**-7
fresh_scale = 2.0**16


def to_half(values, scale):
    return (values.astype(jnp.float32) * scale).astype(jnp.float16)


def from_half(values, scale):
    return (values.astype(jnp.float32) * (1.0 / scale)).astype(jnp.bfloat16)


def gather_by_exchange(block, axis):
    count = lax.axis_size(axis)
    return lax.all_to_all(
        jnp.broadcast_to(block[None], (count,) + block.shape), axis, 0, 0, tiled=True
    )


def shards(
    hidden_rows,
    parent_beam,
    norm_gain,
    route_ids,
    route_weight,
    expert_weight,
    learn_tokens,
    learn_live,
    cotangent,
    master,
    first_moment,
    second_moment,
):
    hid_local = master.shape[2]
    own_rows = master.shape[0]
    wide = 2 * hid_local
    n_y, n_z = lax.axis_size("y"), lax.axis_size("z")
    n_x = lax.axis_size(COLUMN)

    half = learn_tokens.shape[0] // 2
    core = lax.axis_index("core")

    def own_first(block):
        return jnp.concatenate(
            [
                lax.dynamic_slice_in_dim(block, core * half, half, 0),
                lax.dynamic_slice_in_dim(block, (1 - core) * half, half, 0),
            ],
            axis=0,
        )

    own_slice = lax.all_to_all(
        lax.dynamic_slice_in_dim(learn_tokens, core * half, half, 0),
        "y",
        split_axis=1,
        concat_axis=0,
        tiled=True,
    )
    weights = lax.all_gather(
        master.astype(jnp.bfloat16).reshape(own_rows, wide), "z", axis=0, tiled=True
    )
    own_slice, weights = lax.optimization_barrier((own_slice, weights))
    other_slice = lax.ppermute(own_slice, "core", SWAP)
    token_slice = jnp.concatenate([own_slice, other_slice], axis=0)

    rows_dev, width = hidden_rows.shape
    grouped = hidden_rows.reshape(rows_dev // BEAMS, BEAMS, width)
    selector = (
        parent_beam.reshape(rows_dev // BEAMS, BEAMS, 1)
        == jnp.arange(BEAMS, dtype=jnp.int32)[None, None, :]
    ).astype(jnp.bfloat16)
    reordered = jnp.einsum(
        "rbc,rcd->rbd", selector, grouped, preferred_element_type=jnp.float32
    ).reshape(rows_dev, width)
    mean_square = jnp.mean(reordered * reordered, axis=1, keepdims=True)
    normed = (reordered * lax.rsqrt(mean_square + norm_epsilon) * norm_gain[None, :]).astype(
        jnp.bfloat16
    )
    flat_ids = route_ids.reshape(rows_dev * TOP)
    onehot = (flat_ids[:, None] == jnp.arange(EXPERTS, dtype=jnp.int32)[None, :]).astype(jnp.int32)
    earlier = jnp.cumsum(onehot, axis=0) - onehot
    position = jnp.sum(earlier * onehot, axis=1)
    slot_index = flat_ids * CAP + position
    slot_table = (
        slot_index[:, None] == jnp.arange(EXPERTS * CAP, dtype=jnp.int32)[None, :]
    ).astype(jnp.float32)
    row_table = slot_table.reshape(rows_dev, TOP, EXPERTS * CAP).sum(axis=1).astype(jnp.bfloat16)
    share = width // n_x
    normed_share = lax.dynamic_index_in_dim(
        normed.reshape(rows_dev, n_x, share), lax.axis_index(COLUMN), axis=1, keepdims=False
    )
    outgoing = lax.dot_general(
        row_table, normed_share, (((0,), (0,)), ((), ())), preferred_element_type=jnp.float32
    ).astype(jnp.bfloat16)
    outgoing, own_slice = lax.optimization_barrier((outgoing, own_slice))
    arrived = lax.all_to_all(
        outgoing.reshape(n_y * n_z, CAP, share), ROW, split_axis=0, concat_axis=0, tiled=True
    ).reshape(EXPERTS * CAP, share)

    partial_pre = to_half(
        jnp.dot(token_slice, weights, preferred_element_type=jnp.float32), pre_scale
    )
    partial_pre = partial_pre.reshape(2, n_y, half, wide).transpose(1, 0, 2, 3)
    partial_pre, arrived = lax.optimization_barrier((partial_pre, arrived))
    pre_parts = lax.all_to_all(partial_pre, "y", split_axis=0, concat_axis=0, tiled=True)
    projected = jnp.sum(pre_parts.astype(jnp.float32), axis=0).reshape(2 * half, wide) * (
        1.0 / pre_scale
    )
    gate_pre = projected[:, :hid_local]
    up_pre = projected[:, hid_local:]
    sigmoid_gate = jax.nn.sigmoid(gate_pre)
    upstream = own_first(cotangent).astype(jnp.float32) * own_first(
        learn_live.astype(jnp.float32)[:, None]
    )
    slope = sigmoid_gate * (1.0 + gate_pre * (1.0 - sigmoid_gate))
    grad_pre = jnp.concatenate(
        [upstream * up_pre * slope, upstream * gate_pre * sigmoid_gate], axis=1
    ).astype(jnp.bfloat16)

    pieces = [arrived] + [
        lax.ppermute(arrived, ("xl", "xh"), [(i, i ^ k) for i in range(4)]) for k in (1, 2, 3)
    ]
    pieces = jnp.stack(pieces)
    pieces = jnp.stack([pieces, lax.ppermute(pieces, "core", SWAP)])
    local_weight = expert_weight.reshape(2, 2, 2, share, wide)
    for place, axis in enumerate(COLUMN):
        local_weight = jnp.where(
            lax.axis_index(axis) == 1, jnp.flip(local_weight, place), local_weight
        )
    local_weight = local_weight.transpose(1, 0, 2, 3, 4)

    grad_all = gather_by_exchange(grad_pre, "y").reshape(n_y, 2, half, wide)
    grad_all = grad_all.transpose(1, 0, 2, 3).reshape(token_slice.shape[0], wide)
    partial = to_half(
        lax.dot_general(
            token_slice, grad_all, (((0,), (0,)), ((), ())), preferred_element_type=jnp.float32
        ),
        grad_scale,
    )
    parts = lax.all_to_all(
        partial.reshape(n_z, own_rows, wide), "z", split_axis=0, concat_axis=0, tiled=True
    )
    gradient = (jnp.sum(parts.astype(jnp.float32), axis=0) * (1.0 / grad_scale)).reshape(
        master.shape
    )
    new_first = beta_one * first_moment + (1.0 - beta_one) * gradient
    new_second = beta_two * second_moment + (1.0 - beta_two) * gradient * gradient
    correct_one = 1.0 - beta_one**adam_step
    correct_two = 1.0 - beta_two**adam_step
    update = new_first / correct_one / (jnp.sqrt(new_second / correct_two) + epsilon)
    new_master = master - learn_rate * (update + decay_rate * master)
    fresh_rows = to_half(new_master.astype(jnp.bfloat16), fresh_scale)

    projected_rows = jnp.einsum(
        "cjsd,cjdk->sk",
        pieces,
        local_weight.reshape(2, 4, share, wide),
        preferred_element_type=jnp.float32,
    )
    gate_rows = projected_rows[:, :hid_local]
    activated_rows = (
        gate_rows * jax.nn.sigmoid(gate_rows) * projected_rows[:, hid_local:]
    ).astype(jnp.bfloat16)
    activated_rows, fresh_rows = lax.optimization_barrier((activated_rows, fresh_rows))
    returned = lax.all_to_all(
        activated_rows.reshape(n_y * n_z, CAP, hid_local), ROW, split_axis=0, concat_axis=0, tiled=True
    )
    fresh = lax.all_gather(fresh_rows, ROW, axis=0, tiled=True)
    returned, fresh = lax.optimization_barrier((returned, fresh))
    fresh = from_half(fresh, fresh_scale)
    back_slots = returned.reshape(EXPERTS * CAP, hid_local)
    picked = jnp.dot(
        slot_table.astype(jnp.bfloat16), back_slots, preferred_element_type=jnp.float32
    )
    rolled = (
        (picked * route_weight.reshape(rows_dev * TOP, 1))
        .astype(jnp.bfloat16)
        .reshape(rows_dev, TOP, hid_local)
    )
    return (rolled, new_master, new_first, new_second, fresh)


def solution(mesh):
    fine = Mesh(mesh.devices.reshape(2, 2, 8, 8, 2), ("xl", "core", "y", "z", "xh"))
    placed = (
        P(ROW, None),
        P(ROW),
        P(),
        P(ROW, None),
        P(ROW, None),
        P(ROW, None, None, COLUMN),
        P(ROW, None),
        P(ROW),
        P(ROW, COLUMN),
        P(ROW, None, COLUMN),
        P(ROW, None, COLUMN),
        P(ROW, None, COLUMN),
    )
    return jax.shard_map(
        shards,
        mesh=fine,
        in_specs=placed,
        out_specs=(
            P(ROW, None, COLUMN),
            P(ROW, None, COLUMN),
            P(ROW, None, COLUMN),
            P(ROW, None, COLUMN),
            P(None, None, COLUMN),
        ),
        check_vma=False,
    )
```

```python
import jax
import jax.numpy as jnp
from jax import lax
from jax.sharding import Mesh, PartitionSpec as P

EXPERTS = 64
TOP = 8
BEAMS = 4
CAP = 4

beta_one = 0.9
beta_two = 0.95
learn_rate = 0.01
decay_rate = 0.1
epsilon = 1e-08
norm_epsilon = 1e-06
adam_step = 10.0

ROW = ("y", "z")
COLUMN = ("xl", "core", "xh")
ALONG_X = ("xl", "xh")
SWAP = [(0, 1), (1, 0)]
pre_scale = 2.0**7
grad_scale = 2.0**-7
fresh_scale = 2.0**16


def to_half(values, scale):
    return (values.astype(jnp.float32) * scale).astype(jnp.float16)


def from_half(values, scale):
    return (values.astype(jnp.float32) * (1.0 / scale)).astype(jnp.bfloat16)


def gather_by_exchange(block, axis):
    count = lax.axis_size(axis)
    return lax.all_to_all(
        jnp.broadcast_to(block[None], (count,) + block.shape), axis, 0, 0, tiled=True
    )


def shards(
    hidden_rows,
    parent_beam,
    norm_gain,
    route_ids,
    route_weight,
    expert_weight,
    learn_tokens,
    learn_live,
    cotangent,
    master,
    first_moment,
    second_moment,
):
    hid_local = master.shape[2]
    own_rows = master.shape[0]
    wide = 2 * hid_local
    n_y, n_z = lax.axis_size("y"), lax.axis_size("z")

    half = learn_tokens.shape[0] // 2
    core = lax.axis_index("core")

    def own_first(block):
        return jnp.concatenate(
            [
                lax.dynamic_slice_in_dim(block, core * half, half, 0),
                lax.dynamic_slice_in_dim(block, (1 - core) * half, half, 0),
            ],
            axis=0,
        )

    rows_dev, width = hidden_rows.shape
    grouped = hidden_rows.reshape(rows_dev // BEAMS, BEAMS, width)
    selector = (
        parent_beam.reshape(rows_dev // BEAMS, BEAMS, 1)
        == jnp.arange(BEAMS, dtype=jnp.int32)[None, None, :]
    ).astype(jnp.bfloat16)
    reordered = jnp.einsum(
        "rbc,rcd->rbd", selector, grouped, preferred_element_type=jnp.float32
    ).reshape(rows_dev, width)
    mean_square = jnp.mean(reordered * reordered, axis=1, keepdims=True)
    normed = (reordered * lax.rsqrt(mean_square + norm_epsilon) * norm_gain[None, :]).astype(
        jnp.bfloat16
    )
    flat_ids = route_ids.reshape(rows_dev * TOP)
    onehot = (flat_ids[:, None] == jnp.arange(EXPERTS, dtype=jnp.int32)[None, :]).astype(jnp.int32)
    earlier = jnp.cumsum(onehot, axis=0) - onehot
    position = jnp.sum(earlier * onehot, axis=1)
    slot_index = flat_ids * CAP + position
    slot_table = (
        slot_index[:, None] == jnp.arange(EXPERTS * CAP, dtype=jnp.int32)[None, :]
    ).astype(jnp.float32)
    row_table = slot_table.reshape(rows_dev, TOP, EXPERTS, CAP).sum(axis=1)
    slot_row = lax.axis_index(ALONG_X)
    row_table = lax.dynamic_index_in_dim(row_table, slot_row, axis=2, keepdims=False)
    span = width // 2
    normed_half = lax.dynamic_slice_in_dim(normed, core * span, span, 1)
    outgoing = lax.dot_general(
        row_table.astype(jnp.bfloat16),
        normed_half,
        (((0,), (0,)), ((), ())),
        preferred_element_type=jnp.float32,
    ).astype(jnp.bfloat16)
    features = width // n_y
    chunks = span // features
    tokens_half = lax.dynamic_slice_in_dim(learn_tokens, core * half, half, 0)
    along_y = jnp.concatenate(
        [
            tokens_half.reshape(half, n_y, features).transpose(1, 0, 2),
            outgoing.reshape(n_y, n_z * chunks, features),
        ],
        axis=1,
    )
    along_y = lax.all_to_all(along_y, "y", split_axis=0, concat_axis=0, tiled=True)
    weights = lax.all_gather(
        master.astype(jnp.bfloat16).reshape(own_rows, wide), "z", axis=0, tiled=True
    )
    along_y, weights = lax.optimization_barrier((along_y, weights))
    own_slice = along_y[:, :half].reshape(n_y * half, features)
    other_slice = lax.ppermute(own_slice, "core", SWAP)
    token_slice = jnp.concatenate([own_slice, other_slice], axis=0)
    along_z = along_y[:, half:].reshape(n_y, n_z, chunks, features).transpose(1, 0, 2, 3)
    arrived = lax.all_to_all(along_z, "z", split_axis=0, concat_axis=0, tiled=True)
    arrived = arrived.reshape(n_z * n_y, span)

    partial_pre = to_half(
        jnp.dot(token_slice, weights, preferred_element_type=jnp.float32), pre_scale
    )
    partial_pre = partial_pre.reshape(2, n_y, half, wide).transpose(1, 0, 2, 3)
    partial_pre, arrived = lax.optimization_barrier((partial_pre, arrived))
    pre_parts = lax.all_to_all(partial_pre, "y", split_axis=0, concat_axis=0, tiled=True)
    projected = jnp.sum(pre_parts.astype(jnp.float32), axis=0).reshape(2 * half, wide) * (
        1.0 / pre_scale
    )
    gate_pre = projected[:, :hid_local]
    up_pre = projected[:, hid_local:]
    sigmoid_gate = jax.nn.sigmoid(gate_pre)
    upstream = own_first(cotangent).astype(jnp.float32) * own_first(
        learn_live.astype(jnp.float32)[:, None]
    )
    slope = sigmoid_gate * (1.0 + gate_pre * (1.0 - sigmoid_gate))
    grad_pre = jnp.concatenate(
        [upstream * up_pre * slope, upstream * gate_pre * sigmoid_gate], axis=1
    ).astype(jnp.bfloat16)

    pieces = [arrived] + [
        lax.ppermute(arrived, ALONG_X, [(i, i ^ k) for i in range(CAP)]) for k in range(1, CAP)
    ]
    pieces = jnp.concatenate(pieces, axis=0)
    other_pieces = lax.ppermute(pieces, "core", SWAP)
    local_weight = expert_weight.reshape(width, wide)

    grad_all = gather_by_exchange(grad_pre, "y").reshape(n_y, 2, half, wide)
    grad_all = grad_all.transpose(1, 0, 2, 3).reshape(token_slice.shape[0], wide)
    partial = to_half(
        lax.dot_general(
            token_slice, grad_all, (((0,), (0,)), ((), ())), preferred_element_type=jnp.float32
        ),
        grad_scale,
    )
    parts = lax.all_to_all(
        partial.reshape(n_z, own_rows, wide), "z", split_axis=0, concat_axis=0, tiled=True
    )
    gradient = (jnp.sum(parts.astype(jnp.float32), axis=0) * (1.0 / grad_scale)).reshape(
        master.shape
    )
    new_first = beta_one * first_moment + (1.0 - beta_one) * gradient
    new_second = beta_two * second_moment + (1.0 - beta_two) * gradient * gradient
    correct_one = 1.0 - beta_one**adam_step
    correct_two = 1.0 - beta_two**adam_step
    update = new_first / correct_one / (jnp.sqrt(new_second / correct_two) + epsilon)
    new_master = master - learn_rate * (update + decay_rate * master)
    fresh_rows = to_half(new_master.astype(jnp.bfloat16), fresh_scale)

    projected_rows = jnp.dot(
        jnp.where(core == 0, pieces, other_pieces),
        local_weight[:span],
        preferred_element_type=jnp.float32,
    ) + jnp.dot(
        jnp.where(core == 0, other_pieces, pieces),
        local_weight[span:],
        preferred_element_type=jnp.float32,
    )
    gate_rows = projected_rows[:, :hid_local]
    activated_rows = (
        gate_rows * jax.nn.sigmoid(gate_rows) * projected_rows[:, hid_local:]
    ).astype(jnp.bfloat16)
    activated_rows = activated_rows.reshape(2, 2, n_z, n_y, hid_local)
    for place, axis in enumerate(ALONG_X):
        activated_rows = jnp.where(
            lax.axis_index(axis) == 1, jnp.flip(activated_rows, place), activated_rows
        )
    activated_rows = activated_rows.transpose(3, 2, 0, 1, 4).reshape(n_y * n_z, CAP, hid_local)
    fresh_rows = gather_by_exchange(fresh_rows.reshape(own_rows, wide), "z")
    activated_rows, fresh_rows = lax.optimization_barrier((activated_rows, fresh_rows))
    returned = lax.all_to_all(
        activated_rows, ROW, split_axis=0, concat_axis=0, tiled=True
    )
    fresh = lax.all_gather(fresh_rows.reshape(n_z * own_rows, wide), "y", axis=0, tiled=True)
    returned, fresh = lax.optimization_barrier((returned, fresh))
    fresh = from_half(fresh, fresh_scale).reshape(n_y * n_z * own_rows, 2, hid_local)
    back_slots = returned.reshape(EXPERTS * CAP, hid_local)
    picked = jnp.dot(
        slot_table.astype(jnp.bfloat16), back_slots, preferred_element_type=jnp.float32
    )
    rolled = (
        (picked * route_weight.reshape(rows_dev * TOP, 1))
        .astype(jnp.bfloat16)
        .reshape(rows_dev, TOP, hid_local)
    )
    return (rolled, new_master, new_first, new_second, fresh)


def solution(mesh):
    fine = Mesh(mesh.devices.reshape(2, 2, 8, 8, 2), ("xl", "core", "y", "z", "xh"))
    placed = (
        P(ROW, None),
        P(ROW),
        P(),
        P(ROW, None),
        P(ROW, None),
        P(ROW, None, None, COLUMN),
        P(ROW, None),
        P(ROW),
        P(ROW, COLUMN),
        P(ROW, None, COLUMN),
        P(ROW, None, COLUMN),
        P(ROW, None, COLUMN),
    )
    return jax.shard_map(
        shards,
        mesh=fine,
        in_specs=placed,
        out_specs=(
            P(ROW, None, COLUMN),
            P(ROW, None, COLUMN),
            P(ROW, None, COLUMN),
            P(ROW, None, COLUMN),
            P(None, None, COLUMN),
        ),
        check_vma=False,
    )
```

```python
import jax
import jax.numpy as jnp
from jax import lax
from jax.sharding import Mesh, PartitionSpec as P

EXPERTS = 64
TOP = 8
BEAMS = 4
CAP = 4

beta_one = 0.9
beta_two = 0.95
learn_rate = 0.01
decay_rate = 0.1
epsilon = 1e-08
norm_epsilon = 1e-06
adam_step = 10.0

ROW = ("y", "z")
COLUMN = ("xl", "core", "xh")
ALONG_X = ("xl", "xh")
SWAP = [(0, 1), (1, 0)]
pre_scale = 2.0**7
grad_scale = 2.0**-7
fresh_scale = 2.0**16


def to_half(values, scale):
    return (values.astype(jnp.float32) * scale).astype(jnp.float16)


def from_half(values, scale):
    return (values.astype(jnp.float32) * (1.0 / scale)).astype(jnp.bfloat16)


def gather_by_exchange(block, axis):
    count = lax.axis_size(axis)
    return lax.all_to_all(
        jnp.broadcast_to(block[None], (count,) + block.shape), axis, 0, 0, tiled=True
    )


def shards(
    hidden_rows,
    parent_beam,
    norm_gain,
    route_ids,
    route_weight,
    expert_weight,
    learn_tokens,
    learn_live,
    cotangent,
    master,
    first_moment,
    second_moment,
):
    hid_local = master.shape[2]
    own_rows = master.shape[0]
    wide = 2 * hid_local
    n_y, n_z = lax.axis_size("y"), lax.axis_size("z")

    half = learn_tokens.shape[0] // 2
    core = lax.axis_index("core")

    def own_first(block):
        return jnp.concatenate(
            [
                lax.dynamic_slice_in_dim(block, core * half, half, 0),
                lax.dynamic_slice_in_dim(block, (1 - core) * half, half, 0),
            ],
            axis=0,
        )

    rows_dev, width = hidden_rows.shape
    grouped = hidden_rows.reshape(rows_dev // BEAMS, BEAMS, width)
    selector = (
        parent_beam.reshape(rows_dev // BEAMS, BEAMS, 1)
        == jnp.arange(BEAMS, dtype=jnp.int32)[None, None, :]
    ).astype(jnp.bfloat16)
    reordered = jnp.einsum(
        "rbc,rcd->rbd", selector, grouped, preferred_element_type=jnp.float32
    ).reshape(rows_dev, width)
    mean_square = jnp.mean(reordered * reordered, axis=1, keepdims=True)
    normed = (reordered * lax.rsqrt(mean_square + norm_epsilon) * norm_gain[None, :]).astype(
        jnp.bfloat16
    )
    flat_ids = route_ids.reshape(rows_dev * TOP)
    onehot = (flat_ids[:, None] == jnp.arange(EXPERTS, dtype=jnp.int32)[None, :]).astype(jnp.int32)
    earlier = jnp.cumsum(onehot, axis=0) - onehot
    position = jnp.sum(earlier * onehot, axis=1)
    slot_index = flat_ids * CAP + position
    slot_table = (
        slot_index[:, None] == jnp.arange(EXPERTS * CAP, dtype=jnp.int32)[None, :]
    ).astype(jnp.float32)
    row_table = slot_table.reshape(rows_dev, TOP, EXPERTS, CAP).sum(axis=1)
    slot_row = lax.axis_index(ALONG_X)
    row_table = lax.dynamic_index_in_dim(row_table, slot_row, axis=2, keepdims=False)
    span = width // 2
    normed_half = lax.dynamic_slice_in_dim(normed, core * span, span, 1)
    outgoing = lax.dot_general(
        row_table.astype(jnp.bfloat16),
        normed_half,
        (((0,), (0,)), ((), ())),
        preferred_element_type=jnp.float32,
    ).astype(jnp.bfloat16)
    features = width // n_y
    chunks = span // features
    tokens_half = lax.dynamic_slice_in_dim(learn_tokens, core * half, half, 0)
    along_y = jnp.concatenate(
        [
            tokens_half.reshape(half, n_y, features).transpose(1, 0, 2),
            outgoing.reshape(n_y, n_z * chunks, features),
        ],
        axis=1,
    )
    along_y = lax.all_to_all(along_y, "y", split_axis=0, concat_axis=0, tiled=True)
    weights = lax.all_gather(
        master.astype(jnp.bfloat16).reshape(own_rows, wide), "z", axis=0, tiled=True
    )
    along_y, weights = lax.optimization_barrier((along_y, weights))
    own_slice = along_y[:, :half].reshape(n_y * half, features)
    other_slice = lax.ppermute(own_slice, "core", SWAP)
    token_slice = jnp.concatenate([own_slice, other_slice], axis=0)
    along_z = along_y[:, half:].reshape(n_y, n_z, chunks, features).transpose(1, 0, 2, 3)
    arrived = lax.all_to_all(along_z, "z", split_axis=0, concat_axis=0, tiled=True)
    arrived = arrived.reshape(n_z * n_y, span)

    partial_pre = to_half(
        jnp.dot(token_slice, weights, preferred_element_type=jnp.float32), pre_scale
    )
    partial_pre = partial_pre.reshape(2, n_y, half, wide).transpose(1, 0, 2, 3)
    partial_pre, arrived = lax.optimization_barrier((partial_pre, arrived))
    pre_parts = lax.all_to_all(partial_pre, "y", split_axis=0, concat_axis=0, tiled=True)
    pieces = [arrived] + [
        lax.ppermute(arrived, ALONG_X, [(i, i ^ k) for i in range(CAP)]) for k in range(1, CAP)
    ]
    pre_parts, pieces = lax.optimization_barrier((pre_parts, pieces))

    projected = jnp.sum(pre_parts.astype(jnp.float32), axis=0).reshape(2 * half, wide) * (
        1.0 / pre_scale
    )
    gate_pre = projected[:, :hid_local]
    up_pre = projected[:, hid_local:]
    sigmoid_gate = jax.nn.sigmoid(gate_pre)
    upstream = own_first(cotangent).astype(jnp.float32) * own_first(
        learn_live.astype(jnp.float32)[:, None]
    )
    slope = sigmoid_gate * (1.0 + gate_pre * (1.0 - sigmoid_gate))
    grad_pre = jnp.concatenate(
        [upstream * up_pre * slope, upstream * gate_pre * sigmoid_gate], axis=1
    ).astype(jnp.bfloat16)

    grad_all = gather_by_exchange(grad_pre, "y").reshape(n_y, 2, half, wide)
    pieces = jnp.concatenate(pieces, axis=0)
    other_pieces = lax.ppermute(pieces, "core", SWAP)
    grad_all, other_pieces = lax.optimization_barrier((grad_all, other_pieces))
    grad_all = grad_all.transpose(1, 0, 2, 3).reshape(token_slice.shape[0], wide)
    partial = to_half(
        lax.dot_general(
            token_slice, grad_all, (((0,), (0,)), ((), ())), preferred_element_type=jnp.float32
        ),
        grad_scale,
    )
    parts = lax.all_to_all(
        partial.reshape(n_z, own_rows, wide), "z", split_axis=0, concat_axis=0, tiled=True
    )
    gradient = (jnp.sum(parts.astype(jnp.float32), axis=0) * (1.0 / grad_scale)).reshape(
        master.shape
    )
    new_first = beta_one * first_moment + (1.0 - beta_one) * gradient
    new_second = beta_two * second_moment + (1.0 - beta_two) * gradient * gradient
    correct_one = 1.0 - beta_one**adam_step
    correct_two = 1.0 - beta_two**adam_step
    update = new_first / correct_one / (jnp.sqrt(new_second / correct_two) + epsilon)
    new_master = master - learn_rate * (update + decay_rate * master)
    fresh_rows = new_master.astype(jnp.bfloat16).reshape(own_rows, wide)

    local_weight = expert_weight.reshape(width, wide)
    projected_rows = jnp.dot(
        jnp.where(core == 0, pieces, other_pieces),
        local_weight[:span],
        preferred_element_type=jnp.float32,
    ) + jnp.dot(
        jnp.where(core == 0, other_pieces, pieces),
        local_weight[span:],
        preferred_element_type=jnp.float32,
    )
    gate_rows = projected_rows[:, :hid_local]
    activated_rows = (
        gate_rows * jax.nn.sigmoid(gate_rows) * projected_rows[:, hid_local:]
    ).astype(jnp.bfloat16)
    activated_rows = activated_rows.reshape(2, 2, n_z, n_y, hid_local)
    for place, axis in enumerate(ALONG_X):
        activated_rows = jnp.where(
            lax.axis_index(axis) == 1, jnp.flip(activated_rows, place), activated_rows
        )
    activated_rows = activated_rows.transpose(2, 3, 1, 0, 4).reshape(n_z, n_y * 2, wide)
    along_z = jnp.concatenate(
        [jnp.broadcast_to(fresh_rows[None], (n_z,) + fresh_rows.shape), activated_rows], axis=1
    )
    along_z = lax.all_to_all(along_z, "z", split_axis=0, concat_axis=0, tiled=True)
    fresh_rows = to_half(along_z[:, :own_rows].reshape(n_z * own_rows, wide), fresh_scale)
    along_y = along_z[:, own_rows:].reshape(n_z, n_y, 2, wide).transpose(1, 0, 2, 3)
    returned = lax.all_to_all(along_y, "y", split_axis=0, concat_axis=0, tiled=True)
    fresh = lax.all_gather(fresh_rows, "y", axis=0, tiled=True)
    returned, fresh = lax.optimization_barrier((returned, fresh))
    fresh = from_half(fresh, fresh_scale).reshape(n_y * n_z * own_rows, 2, hid_local)
    back_slots = returned.reshape(EXPERTS, 2, 2, hid_local).transpose(0, 2, 1, 3)
    back_slots = back_slots.reshape(EXPERTS * CAP, hid_local)
    picked = jnp.dot(
        slot_table.astype(jnp.bfloat16), back_slots, preferred_element_type=jnp.float32
    )
    rolled = (
        (picked * route_weight.reshape(rows_dev * TOP, 1))
        .astype(jnp.bfloat16)
        .reshape(rows_dev, TOP, hid_local)
    )
    return (rolled, new_master, new_first, new_second, fresh)


def solution(mesh):
    fine = Mesh(mesh.devices.reshape(2, 2, 8, 8, 2), ("xl", "core", "y", "z", "xh"))
    placed = (
        P(ROW, None),
        P(ROW),
        P(),
        P(ROW, None),
        P(ROW, None),
        P(ROW, None, None, COLUMN),
        P(ROW, None),
        P(ROW),
        P(ROW, COLUMN),
        P(ROW, None, COLUMN),
        P(ROW, None, COLUMN),
        P(ROW, None, COLUMN),
    )
    return jax.shard_map(
        shards,
        mesh=fine,
        in_specs=placed,
        out_specs=(
            P(ROW, None, COLUMN),
            P(ROW, None, COLUMN),
            P(ROW, None, COLUMN),
            P(ROW, None, COLUMN),
            P(None, None, COLUMN),
        ),
        check_vma=False,
    )
```

```python
import jax
import jax.numpy as jnp
from jax import lax
from jax.experimental import pallas as pl
from jax.experimental.pallas import tpu as pltpu
from jax.sharding import Mesh, PartitionSpec as P

EXPERTS = 64
TOP = 8
BEAMS = 4
CAP = 4

beta_one = 0.9
beta_two = 0.95
learn_rate = 0.01
decay_rate = 0.1
epsilon = 1e-08
norm_epsilon = 1e-06
adam_step = 10.0

ROW = ("y", "z")
COLUMN = ("xl", "core", "xh")
ALONG_X = ("xl", "xh")
SWAP = [(0, 1), (1, 0)]
pre_scale = 2.0**7
fresh_scale = 2.0**16


def to_half(values, scale):
    return (values.astype(jnp.float32) * scale).astype(jnp.float16)


def from_half(values, scale):
    return (values.astype(jnp.float32) * (1.0 / scale)).astype(jnp.bfloat16)


def gather_by_exchange(block, axis):
    count = lax.axis_size(axis)
    return lax.all_to_all(
        jnp.broadcast_to(block[None], (count,) + block.shape), axis, 0, 0, tiled=True
    )


def stack_kernel(*refs):
    blocks, stacked = refs[:-1], refs[-1]
    rows = blocks[0].shape[0]
    for k, block in enumerate(blocks):
        stacked[k * rows : (k + 1) * rows] = block[...]


def stack_rows(blocks):
    rows, columns = blocks[0].shape
    count = len(blocks)
    return pl.pallas_call(
        stack_kernel,
        out_shape=jax.ShapeDtypeStruct((count * rows, columns), blocks[0].dtype),
        in_specs=[pl.BlockSpec(memory_space=pltpu.VMEM)] * count,
        out_specs=pl.BlockSpec(memory_space=pltpu.VMEM),
        compiler_params=pltpu.CompilerParams(vmem_limit_bytes=16 * 1024 * 1024),
        name="stack_rows",
        cost_estimate=pl.CostEstimate(
            flops=0, bytes_accessed=4 * count * rows * columns, transcendentals=0
        ),
    )(*blocks)


def route_kernel(hidden_ref, beam_ref, gain_ref, ids_ref, out_ref):
    rows, width = hidden_ref.shape
    core = lax.axis_index("core")
    slot = (lax.axis_index("xl") * 2 + lax.axis_index("xh")).astype(jnp.float32)
    hidden = hidden_ref[...].astype(jnp.float32)
    mean_square = jnp.mean(hidden * hidden, axis=1, keepdims=True)
    normed = (hidden * lax.rsqrt(mean_square + norm_epsilon) * gain_ref[...]).astype(jnp.bfloat16)
    ids = ids_ref[...]
    expert = lax.broadcasted_iota(jnp.int32, (EXPERTS, rows), 0)
    named = jnp.zeros((EXPERTS, rows), jnp.float32)
    for k in range(TOP):
        named = named + (expert == ids[k : k + 1, :]).astype(jnp.float32)
    first = lax.broadcasted_iota(jnp.int32, (rows, rows), 0)
    second = lax.broadcasted_iota(jnp.int32, (rows, rows), 1)
    earlier = jnp.dot(
        named, (first < second).astype(jnp.float32), preferred_element_type=jnp.float32
    )
    sends = jnp.where(earlier == slot, named, 0.0)
    parent = second - (second & (BEAMS - 1)) + beam_ref[...]
    source = (first == parent).astype(jnp.float32)
    table = lax.dot_general(
        sends, source, (((1,), (1,)), ((), ())), preferred_element_type=jnp.float32
    ).astype(jnp.bfloat16)

    @pl.when(core == 0)
    def _():
        out_ref[...] = jnp.dot(
            table, normed[:, : width // 2], preferred_element_type=jnp.float32
        ).astype(jnp.bfloat16)

    @pl.when(core != 0)
    def _():
        out_ref[...] = jnp.dot(
            table, normed[:, width // 2 :], preferred_element_type=jnp.float32
        ).astype(jnp.bfloat16)


def route_rows(hidden_rows, parent_beam, norm_gain, route_ids):
    rows, width = hidden_rows.shape
    return pl.pallas_call(
        route_kernel,
        out_shape=jax.ShapeDtypeStruct((EXPERTS, width // 2), jnp.bfloat16),
        in_specs=[pl.BlockSpec(memory_space=pltpu.VMEM)] * 4,
        out_specs=pl.BlockSpec(memory_space=pltpu.VMEM),
        compiler_params=pltpu.CompilerParams(vmem_limit_bytes=16 * 1024 * 1024),
        name="route_rows",
        cost_estimate=pl.CostEstimate(
            flops=2 * EXPERTS * rows * width, bytes_accessed=1 << 19, transcendentals=rows
        ),
    )(hidden_rows, parent_beam.reshape(1, rows), norm_gain.reshape(1, width), route_ids.T)


def shards(
    hidden_rows,
    parent_beam,
    norm_gain,
    route_ids,
    route_weight,
    expert_weight,
    learn_tokens,
    learn_live,
    cotangent,
    master,
    first_moment,
    second_moment,
):
    hid_local = master.shape[2]
    own_rows = master.shape[0]
    wide = 2 * hid_local
    n_y, n_z = lax.axis_size("y"), lax.axis_size("z")

    half = learn_tokens.shape[0] // 2
    core = lax.axis_index("core")

    def own_first(block):
        return jnp.concatenate(
            [
                lax.dynamic_slice_in_dim(block, core * half, half, 0),
                lax.dynamic_slice_in_dim(block, (1 - core) * half, half, 0),
            ],
            axis=0,
        )

    rows_dev, width = hidden_rows.shape
    flat_ids = route_ids.reshape(rows_dev * TOP)
    onehot = (flat_ids[:, None] == jnp.arange(EXPERTS, dtype=jnp.int32)[None, :]).astype(jnp.int32)
    earlier = jnp.cumsum(onehot, axis=0) - onehot
    position = jnp.sum(earlier * onehot, axis=1)
    slot_index = flat_ids * CAP + position
    slot_table = (
        slot_index[:, None] == jnp.arange(EXPERTS * CAP, dtype=jnp.int32)[None, :]
    ).astype(jnp.float32)
    span = width // 2
    outgoing = route_rows(hidden_rows, parent_beam, norm_gain, route_ids)
    features = width // n_y
    chunks = span // features
    tokens_half = lax.dynamic_slice_in_dim(learn_tokens, core * half, half, 0)
    along_y = jnp.concatenate(
        [
            tokens_half.reshape(half, n_y, features).transpose(1, 0, 2),
            outgoing.reshape(n_y, n_z * chunks, features),
        ],
        axis=1,
    )
    along_y = lax.all_to_all(along_y, "y", split_axis=0, concat_axis=0, tiled=True)
    local_weight = expert_weight.reshape(width, wide)
    along_y, local_weight = lax.optimization_barrier((along_y, local_weight))
    own_slice = along_y[:, :half]
    other_slice = lax.ppermute(own_slice, "core", SWAP)
    token_slice = jnp.concatenate([own_slice, other_slice], axis=1)
    token_slice = token_slice.reshape(n_y * 2 * half, features)
    lanes = 2 * wide
    tall = n_z * chunks
    routed = along_y[:, half:].reshape(n_y, n_z, chunks, features).transpose(1, 0, 2, 3)
    routed = jnp.pad(
        routed.reshape(n_z, n_y * chunks, features), ((0, 0), (0, 0), (0, lanes - features))
    )
    low = master.astype(jnp.bfloat16).reshape(own_rows, wide)
    low = jnp.concatenate(
        [low[:tall], jnp.pad(low[tall:], ((0, 2 * tall - own_rows), (0, 0)))], axis=1
    )
    along_z = jnp.concatenate([routed, jnp.broadcast_to(low[None], (n_z,) + low.shape)], axis=1)
    along_z = lax.all_to_all(along_z, "z", split_axis=0, concat_axis=0, tiled=True)
    arrived = along_z[:, : n_y * chunks, :features].reshape(n_z * n_y, span)
    weights = jnp.concatenate(
        [
            along_z[:, n_y * chunks :, :wide],
            along_z[:, n_y * chunks : n_y * chunks + own_rows - tall, wide:],
        ],
        axis=1,
    ).reshape(n_z * own_rows, wide)

    partial_pre = to_half(
        jnp.dot(token_slice, weights, preferred_element_type=jnp.float32), pre_scale
    )
    partial_pre = partial_pre.reshape(n_y, 2 * half, wide)
    pre_parts = lax.all_to_all(partial_pre, "y", split_axis=0, concat_axis=0, tiled=True)
    pieces = [arrived] + [
        lax.ppermute(arrived, ALONG_X, [(i, i ^ k) for i in range(CAP)]) for k in range(1, CAP)
    ]
    projected = jnp.sum(pre_parts.astype(jnp.float32), axis=0) * (1.0 / pre_scale)
    gate_pre = projected[:, :hid_local]
    up_pre = projected[:, hid_local:]
    sigmoid_gate = jax.nn.sigmoid(gate_pre)
    upstream = own_first(cotangent).astype(jnp.float32) * own_first(
        learn_live.astype(jnp.float32)[:, None]
    )
    slope = sigmoid_gate * (1.0 + gate_pre * (1.0 - sigmoid_gate))
    grad_pre = jnp.concatenate(
        [upstream * up_pre * slope, upstream * gate_pre * sigmoid_gate], axis=1
    ).astype(jnp.bfloat16)

    grad_all = gather_by_exchange(grad_pre, "y").reshape(token_slice.shape[0], wide)
    pieces, _ = lax.optimization_barrier((pieces, grad_pre))
    pieces = stack_rows(pieces)
    other_pieces = lax.ppermute(pieces, "core", SWAP)
    projected_rows = jnp.dot(
        jnp.where(core == 0, pieces, other_pieces),
        local_weight[:span],
        preferred_element_type=jnp.float32,
    ) + jnp.dot(
        jnp.where(core == 0, other_pieces, pieces),
        local_weight[span:],
        preferred_element_type=jnp.float32,
    )
    gate_rows = projected_rows[:, :hid_local]
    activated_rows = (
        gate_rows * jax.nn.sigmoid(gate_rows) * projected_rows[:, hid_local:]
    ).astype(jnp.bfloat16)
    activated_rows = activated_rows.reshape(2, 2, n_z, n_y, hid_local)
    for place, axis in enumerate(ALONG_X):
        activated_rows = jnp.where(
            lax.axis_index(axis) == 1, jnp.flip(activated_rows, place), activated_rows
        )
    activated_rows = activated_rows.transpose(2, 3, 1, 0, 4).reshape(n_z, n_y * 2, wide)
    grad_all, activated_rows = lax.optimization_barrier((grad_all, activated_rows))
    partial = lax.dot_general(
        token_slice, grad_all, (((0,), (0,)), ((), ())), preferred_element_type=jnp.float32
    ).astype(jnp.bfloat16)
    along_z = jnp.concatenate([partial.reshape(n_z, own_rows, wide), activated_rows], axis=1)
    along_z = lax.all_to_all(along_z, "z", split_axis=0, concat_axis=0, tiled=True)
    gradient = jnp.sum(along_z[:, :own_rows].astype(jnp.float32), axis=0).reshape(master.shape)
    returned = along_z[:, own_rows:].reshape(n_z, n_y, 2, wide).transpose(1, 0, 2, 3)
    new_first = beta_one * first_moment + (1.0 - beta_one) * gradient
    new_second = beta_two * second_moment + (1.0 - beta_two) * gradient * gradient
    correct_one = 1.0 - beta_one**adam_step
    correct_two = 1.0 - beta_two**adam_step
    update = new_first / correct_one / (jnp.sqrt(new_second / correct_two) + epsilon)
    new_master = master - learn_rate * (update + decay_rate * master)
    fresh_rows = new_master.astype(jnp.bfloat16).reshape(own_rows, wide)

    along_y = jnp.concatenate(
        [
            jnp.broadcast_to(fresh_rows[None], (n_y,) + fresh_rows.shape),
            returned.reshape(n_y, n_z * 2, wide),
        ],
        axis=1,
    )
    along_y = lax.all_to_all(along_y, "y", split_axis=0, concat_axis=0, tiled=True)
    fresh_rows = to_half(along_y[:, :own_rows].reshape(n_y * own_rows, wide), fresh_scale)
    returned = along_y[:, own_rows:]
    fresh = lax.all_gather(fresh_rows, "z", axis=0, tiled=True)
    fresh = from_half(fresh, fresh_scale).reshape(n_z, n_y, own_rows, wide)
    fresh = fresh.transpose(1, 0, 2, 3).reshape(n_y * n_z * own_rows, wide)
    fresh = lax.optimization_barrier(fresh).reshape(n_y * n_z * own_rows, 2, hid_local)
    back_slots = returned.reshape(EXPERTS, 2, 2, hid_local).transpose(0, 2, 1, 3)
    back_slots = back_slots.reshape(EXPERTS * CAP, hid_local)
    picked = jnp.dot(
        slot_table.astype(jnp.bfloat16), back_slots, preferred_element_type=jnp.float32
    )
    rolled = (
        (picked * route_weight.reshape(rows_dev * TOP, 1))
        .astype(jnp.bfloat16)
        .reshape(rows_dev, TOP, hid_local)
    )
    return (rolled, new_master, new_first, new_second, fresh)


def solution(mesh):
    fine = Mesh(mesh.devices.reshape(2, 2, 8, 8, 2), ("xl", "core", "y", "z", "xh"))
    placed = (
        P(ROW, None),
        P(ROW),
        P(),
        P(ROW, None),
        P(ROW, None),
        P(ROW, None, None, COLUMN),
        P(ROW, None),
        P(ROW),
        P(ROW, COLUMN),
        P(ROW, None, COLUMN),
        P(ROW, None, COLUMN),
        P(ROW, None, COLUMN),
    )
    return jax.shard_map(
        shards,
        mesh=fine,
        in_specs=placed,
        out_specs=(
            P(ROW, None, COLUMN),
            P(ROW, None, COLUMN),
            P(ROW, None, COLUMN),
            P(ROW, None, COLUMN),
            P(None, None, COLUMN),
        ),
        check_vma=False,
    )
```

```python
import jax
import jax.numpy as jnp
from jax import lax
from jax.experimental import pallas as pl
from jax.experimental.pallas import tpu as pltpu
from jax.sharding import Mesh, PartitionSpec as P

EXPERTS = 64
TOP = 8
BEAMS = 4
CAP = 4

beta_one = 0.9
beta_two = 0.95
learn_rate = 0.01
decay_rate = 0.1
epsilon = 1e-08
norm_epsilon = 1e-06
adam_step = 10.0

ROW = ("y", "z")
COLUMN = ("xl", "core", "xh")
ALONG_X = ("xl", "xh")
SWAP = [(0, 1), (1, 0)]
pre_scale = 2.0**7
fresh_scale = 2.0**16


def to_half(values, scale):
    return (values.astype(jnp.float32) * scale).astype(jnp.float16)


def from_half(values, scale):
    return (values.astype(jnp.float32) * (1.0 / scale)).astype(jnp.bfloat16)


def gather_by_exchange(block, axis):
    count = lax.axis_size(axis)
    return lax.all_to_all(
        jnp.broadcast_to(block[None], (count,) + block.shape), axis, 0, 0, tiled=True
    )


def stack_kernel(*refs):
    blocks, stacked = refs[:-1], refs[-1]
    rows = blocks[0].shape[1]
    for k, block in enumerate(blocks):
        stacked[:, k * rows : (k + 1) * rows] = block[...]


def stack_rows(blocks):
    outer, rows, columns = blocks[0].shape
    count = len(blocks)
    return pl.pallas_call(
        stack_kernel,
        out_shape=jax.ShapeDtypeStruct((outer, count * rows, columns), blocks[0].dtype),
        in_specs=[pl.BlockSpec(memory_space=pltpu.VMEM)] * count,
        out_specs=pl.BlockSpec(memory_space=pltpu.VMEM),
        compiler_params=pltpu.CompilerParams(vmem_limit_bytes=4 * 1024 * 1024),
        name="stack_rows",
        cost_estimate=pl.CostEstimate(
            flops=0, bytes_accessed=4 * count * outer * rows * columns, transcendentals=0
        ),
    )(*blocks)


def with_neighbours(block):
    return [block] + [
        lax.ppermute(block, ALONG_X, [(i, i ^ k) for i in range(4)]) for k in range(1, 4)
    ]


def route_kernel(hidden_ref, beam_ref, gain_ref, ids_ref, out_ref):
    rows, width = hidden_ref.shape
    core = lax.axis_index("core")
    slot = (lax.axis_index("xl") * 2 + lax.axis_index("xh")).astype(jnp.float32)
    hidden = hidden_ref[...].astype(jnp.float32)
    mean_square = jnp.mean(hidden * hidden, axis=1, keepdims=True)
    normed = (hidden * lax.rsqrt(mean_square + norm_epsilon) * gain_ref[...]).astype(jnp.bfloat16)
    ids = ids_ref[...]
    expert = lax.broadcasted_iota(jnp.int32, (EXPERTS, rows), 0)
    named = jnp.zeros((EXPERTS, rows), jnp.float32)
    for k in range(TOP):
        named = named + (expert == ids[k : k + 1, :]).astype(jnp.float32)
    first = lax.broadcasted_iota(jnp.int32, (rows, rows), 0)
    second = lax.broadcasted_iota(jnp.int32, (rows, rows), 1)
    earlier = jnp.dot(
        named, (first < second).astype(jnp.float32), preferred_element_type=jnp.float32
    )
    sends = jnp.where(earlier == slot, named, 0.0)
    parent = second - (second & (BEAMS - 1)) + beam_ref[...]
    source = (first == parent).astype(jnp.float32)
    table = lax.dot_general(
        sends, source, (((1,), (1,)), ((), ())), preferred_element_type=jnp.float32
    ).astype(jnp.bfloat16)

    @pl.when(core == 0)
    def _():
        out_ref[...] = jnp.dot(
            table, normed[:, : width // 2], preferred_element_type=jnp.float32
        ).astype(jnp.bfloat16)

    @pl.when(core != 0)
    def _():
        out_ref[...] = jnp.dot(
            table, normed[:, width // 2 :], preferred_element_type=jnp.float32
        ).astype(jnp.bfloat16)


def route_rows(hidden_rows, parent_beam, norm_gain, route_ids):
    rows, width = hidden_rows.shape
    return pl.pallas_call(
        route_kernel,
        out_shape=jax.ShapeDtypeStruct((EXPERTS, width // 2), jnp.bfloat16),
        in_specs=[pl.BlockSpec(memory_space=pltpu.VMEM)] * 4,
        out_specs=pl.BlockSpec(memory_space=pltpu.VMEM),
        compiler_params=pltpu.CompilerParams(vmem_limit_bytes=4 * 1024 * 1024),
        name="route_rows",
        cost_estimate=pl.CostEstimate(
            flops=2 * EXPERTS * rows * width, bytes_accessed=1 << 19, transcendentals=rows
        ),
    )(hidden_rows, parent_beam.reshape(1, rows), norm_gain.reshape(1, width), route_ids.T)


def shards(
    hidden_rows,
    parent_beam,
    norm_gain,
    route_ids,
    route_weight,
    expert_weight,
    learn_tokens,
    learn_live,
    cotangent,
    master,
    first_moment,
    second_moment,
):
    hid_local = master.shape[2]
    own_rows = master.shape[0]
    wide = 2 * hid_local
    n_y, n_z = lax.axis_size("y"), lax.axis_size("z")

    tokens = learn_tokens.shape[0]
    quarter = tokens // 4
    core = lax.axis_index("core")

    def own_first(block):
        block = block.reshape(2, 2, quarter, block.shape[1])
        for place, axis in enumerate(("core", "xl")):
            block = jnp.where(lax.axis_index(axis) == 1, jnp.flip(block, place), block)
        return block.reshape(tokens, block.shape[3])

    rows_dev, width = hidden_rows.shape
    flat_ids = route_ids.reshape(rows_dev * TOP)
    onehot = (flat_ids[:, None] == jnp.arange(EXPERTS, dtype=jnp.int32)[None, :]).astype(jnp.int32)
    earlier = jnp.cumsum(onehot, axis=0) - onehot
    position = jnp.sum(earlier * onehot, axis=1)
    slot_index = flat_ids * CAP + position
    slot_table = (
        slot_index[:, None] == jnp.arange(EXPERTS * CAP, dtype=jnp.int32)[None, :]
    ).astype(jnp.float32)
    span = width // 2
    outgoing = route_rows(hidden_rows, parent_beam, norm_gain, route_ids)
    features = width // n_y
    chunks = span // features
    tokens_part = lax.dynamic_slice_in_dim(
        learn_tokens, lax.axis_index(("core", "xl")) * quarter, quarter, 0
    )
    along_y = jnp.concatenate(
        [
            tokens_part.reshape(quarter, n_y, features).transpose(1, 0, 2),
            outgoing.reshape(n_y, n_z * chunks, features),
        ],
        axis=1,
    )
    along_y = lax.all_to_all(along_y, "y", split_axis=0, concat_axis=0, tiled=True)
    local_weight = expert_weight.reshape(width, wide)
    along_y, local_weight = lax.optimization_barrier((along_y, local_weight))
    own_slice = along_y[:, :quarter]
    own_slice = stack_rows([own_slice, lax.ppermute(own_slice, "xl", SWAP)])
    other_slice = lax.ppermute(own_slice, "core", SWAP)
    token_slice = jnp.concatenate([own_slice, other_slice], axis=1).reshape(n_y * tokens, features)
    lanes = 2 * wide
    tall = n_z * chunks
    routed = along_y[:, quarter:].reshape(n_y, n_z, chunks, features).transpose(1, 0, 2, 3)
    routed = jnp.pad(
        routed.reshape(n_z, n_y * chunks, features), ((0, 0), (0, 0), (0, lanes - features))
    )
    low = master.astype(jnp.bfloat16).reshape(own_rows, wide)
    low = jnp.concatenate(
        [low[:tall], jnp.pad(low[tall:], ((0, 2 * tall - own_rows), (0, 0)))], axis=1
    )
    along_z = jnp.concatenate([routed, jnp.broadcast_to(low[None], (n_z,) + low.shape)], axis=1)
    along_z = lax.all_to_all(along_z, "z", split_axis=0, concat_axis=0, tiled=True)
    arrived = along_z[:, : n_y * chunks, :features].reshape(n_z * n_y, span)
    weights = jnp.concatenate(
        [
            along_z[:, n_y * chunks :, :wide],
            along_z[:, n_y * chunks : n_y * chunks + own_rows - tall, wide:],
        ],
        axis=1,
    ).reshape(n_z * own_rows, wide)

    partial_pre = to_half(
        jnp.dot(token_slice, weights, preferred_element_type=jnp.float32), pre_scale
    )
    partial_pre = partial_pre.reshape(n_y, tokens, wide)
    pre_parts = lax.all_to_all(partial_pre, "y", split_axis=0, concat_axis=0, tiled=True)
    pieces = with_neighbours(arrived[None])
    projected = jnp.sum(pre_parts.astype(jnp.float32), axis=0) * (1.0 / pre_scale)
    gate_pre = projected[:, :hid_local]
    up_pre = projected[:, hid_local:]
    sigmoid_gate = jax.nn.sigmoid(gate_pre)
    upstream = own_first(cotangent).astype(jnp.float32) * own_first(
        learn_live.astype(jnp.float32)[:, None]
    )
    slope = sigmoid_gate * (1.0 + gate_pre * (1.0 - sigmoid_gate))
    grad_pre = jnp.concatenate(
        [upstream * up_pre * slope, upstream * gate_pre * sigmoid_gate], axis=1
    ).astype(jnp.bfloat16)

    grad_all = gather_by_exchange(grad_pre, "y").reshape(token_slice.shape[0], wide)
    pieces = stack_rows(pieces)[0]
    other_pieces = lax.ppermute(pieces, "core", SWAP)
    projected_rows = jnp.dot(
        jnp.where(core == 0, pieces, other_pieces),
        local_weight[:span],
        preferred_element_type=jnp.float32,
    ) + jnp.dot(
        jnp.where(core == 0, other_pieces, pieces),
        local_weight[span:],
        preferred_element_type=jnp.float32,
    )
    gate_rows = projected_rows[:, :hid_local]
    activated_rows = (
        gate_rows * jax.nn.sigmoid(gate_rows) * projected_rows[:, hid_local:]
    ).astype(jnp.bfloat16)
    activated_rows = activated_rows.reshape(2, 2, n_z, n_y, hid_local)
    for place, axis in enumerate(ALONG_X):
        activated_rows = jnp.where(
            lax.axis_index(axis) == 1, jnp.flip(activated_rows, place), activated_rows
        )
    activated_rows = activated_rows.transpose(2, 3, 1, 0, 4).reshape(n_z, n_y * 2, wide)
    grad_all, activated_rows = lax.optimization_barrier((grad_all, activated_rows))
    partial = lax.dot_general(
        token_slice, grad_all, (((0,), (0,)), ((), ())), preferred_element_type=jnp.float32
    ).astype(jnp.bfloat16)
    along_z = jnp.concatenate([partial.reshape(n_z, own_rows, wide), activated_rows], axis=1)
    along_z = lax.all_to_all(along_z, "z", split_axis=0, concat_axis=0, tiled=True)
    gradient = jnp.sum(along_z[:, :own_rows].astype(jnp.float32), axis=0).reshape(master.shape)
    returned = along_z[:, own_rows:].reshape(n_z, n_y, 2, wide).transpose(1, 0, 2, 3)
    new_first = beta_one * first_moment + (1.0 - beta_one) * gradient
    new_second = beta_two * second_moment + (1.0 - beta_two) * gradient * gradient
    correct_one = 1.0 - beta_one**adam_step
    correct_two = 1.0 - beta_two**adam_step
    update = new_first / correct_one / (jnp.sqrt(new_second / correct_two) + epsilon)
    new_master = master - learn_rate * (update + decay_rate * master)
    fresh_rows = new_master.astype(jnp.bfloat16).reshape(own_rows, wide)

    along_y = jnp.concatenate(
        [
            jnp.broadcast_to(fresh_rows[None], (n_y,) + fresh_rows.shape),
            returned.reshape(n_y, n_z * 2, wide),
        ],
        axis=1,
    )
    along_y = lax.all_to_all(along_y, "y", split_axis=0, concat_axis=0, tiled=True)
    fresh_rows = to_half(along_y[:, :own_rows].reshape(n_y * own_rows, wide), fresh_scale)
    returned = along_y[:, own_rows:]
    fresh = lax.all_gather(fresh_rows, "z", axis=0, tiled=True)
    fresh = from_half(fresh, fresh_scale).reshape(n_z, n_y, own_rows, wide)
    fresh = fresh.transpose(1, 0, 2, 3).reshape(n_y * n_z * own_rows, wide)
    fresh = lax.optimization_barrier(fresh).reshape(n_y * n_z * own_rows, 2, hid_local)
    back_slots = returned.reshape(EXPERTS, 2, 2, hid_local).transpose(0, 2, 1, 3)
    back_slots = back_slots.reshape(EXPERTS * CAP, hid_local)
    picked = jnp.dot(
        slot_table.astype(jnp.bfloat16), back_slots, preferred_element_type=jnp.float32
    )
    rolled = (
        (picked * route_weight.reshape(rows_dev * TOP, 1))
        .astype(jnp.bfloat16)
        .reshape(rows_dev, TOP, hid_local)
    )
    return (rolled, new_master, new_first, new_second, fresh)


def solution(mesh):
    fine = Mesh(mesh.devices.reshape(2, 2, 8, 8, 2), ("xl", "core", "y", "z", "xh"))
    placed = (
        P(ROW, None),
        P(ROW),
        P(),
        P(ROW, None),
        P(ROW, None),
        P(ROW, None, None, COLUMN),
        P(ROW, None),
        P(ROW),
        P(ROW, COLUMN),
        P(ROW, None, COLUMN),
        P(ROW, None, COLUMN),
        P(ROW, None, COLUMN),
    )
    return jax.shard_map(
        shards,
        mesh=fine,
        in_specs=placed,
        out_specs=(
            P(ROW, None, COLUMN),
            P(ROW, None, COLUMN),
            P(ROW, None, COLUMN),
            P(ROW, None, COLUMN),
            P(None, None, COLUMN),
        ),
        check_vma=False,
    )
```

```python
import jax
import jax.numpy as jnp
from jax import lax
from jax.experimental import pallas as pl
from jax.experimental.pallas import tpu as pltpu
from jax.sharding import Mesh, PartitionSpec as P

EXPERTS = 64
TOP = 8
BEAMS = 4
CAP = 4

beta_one = 0.9
beta_two = 0.95
learn_rate = 0.01
decay_rate = 0.1
epsilon = 1e-08
norm_epsilon = 1e-06
adam_step = 10.0

ROW = ("y", "z")
COLUMN = ("xl", "core", "xh")
ALONG_X = ("xl", "xh")
SWAP = [(0, 1), (1, 0)]
pre_scale = 2.0**7
fresh_scale = 2.0**16


def to_half(values, scale):
    return (values.astype(jnp.float32) * scale).astype(jnp.float16)


def from_half(values, scale):
    return (values.astype(jnp.float32) * (1.0 / scale)).astype(jnp.bfloat16)


def gather_by_exchange(block, axis):
    count = lax.axis_size(axis)
    return lax.all_to_all(
        jnp.broadcast_to(block[None], (count,) + block.shape), axis, 0, 0, tiled=True
    )


def stack_kernel(*refs):
    blocks, stacked = refs[:-1], refs[-1]
    rows = blocks[0].shape[1]
    for k, block in enumerate(blocks):
        stacked[:, k * rows : (k + 1) * rows] = block[...]


def stack_rows(blocks):
    outer, rows, columns = blocks[0].shape
    count = len(blocks)
    return pl.pallas_call(
        stack_kernel,
        out_shape=jax.ShapeDtypeStruct((outer, count * rows, columns), blocks[0].dtype),
        in_specs=[pl.BlockSpec(memory_space=pltpu.VMEM)] * count,
        out_specs=pl.BlockSpec(memory_space=pltpu.VMEM),
        compiler_params=pltpu.CompilerParams(vmem_limit_bytes=4 * 1024 * 1024),
        name="stack_rows",
        cost_estimate=pl.CostEstimate(
            flops=0, bytes_accessed=4 * count * outer * rows * columns, transcendentals=0
        ),
    )(*blocks)


def with_neighbours(block):
    return [block] + [
        lax.ppermute(block, ALONG_X, [(i, i ^ k) for i in range(4)]) for k in range(1, 4)
    ]


def route_kernel(hidden_ref, beam_ref, gain_ref, ids_ref, out_ref):
    rows, width = hidden_ref.shape
    core = lax.axis_index("core")
    slot = (lax.axis_index("xl") * 2 + lax.axis_index("xh")).astype(jnp.float32)
    hidden = hidden_ref[...].astype(jnp.float32)
    mean_square = jnp.mean(hidden * hidden, axis=1, keepdims=True)
    normed = (hidden * lax.rsqrt(mean_square + norm_epsilon) * gain_ref[...]).astype(jnp.bfloat16)
    ids = ids_ref[...]
    expert = lax.broadcasted_iota(jnp.int32, (EXPERTS, rows), 0)
    named = jnp.zeros((EXPERTS, rows), jnp.float32)
    for k in range(TOP):
        named = named + (expert == ids[k : k + 1, :]).astype(jnp.float32)
    first = lax.broadcasted_iota(jnp.int32, (rows, rows), 0)
    second = lax.broadcasted_iota(jnp.int32, (rows, rows), 1)
    earlier = jnp.dot(
        named, (first < second).astype(jnp.float32), preferred_element_type=jnp.float32
    )
    sends = jnp.where(earlier == slot, named, 0.0)
    parent = second - (second & (BEAMS - 1)) + beam_ref[...]
    source = (first == parent).astype(jnp.float32)
    table = lax.dot_general(
        sends, source, (((1,), (1,)), ((), ())), preferred_element_type=jnp.float32
    ).astype(jnp.bfloat16)

    @pl.when(core == 0)
    def _():
        out_ref[...] = jnp.dot(
            table, normed[:, : width // 2], preferred_element_type=jnp.float32
        ).astype(jnp.bfloat16)

    @pl.when(core != 0)
    def _():
        out_ref[...] = jnp.dot(
            table, normed[:, width // 2 :], preferred_element_type=jnp.float32
        ).astype(jnp.bfloat16)


def route_rows(hidden_rows, parent_beam, norm_gain, route_ids):
    rows, width = hidden_rows.shape
    return pl.pallas_call(
        route_kernel,
        out_shape=jax.ShapeDtypeStruct((EXPERTS, width // 2), jnp.bfloat16),
        in_specs=[pl.BlockSpec(memory_space=pltpu.VMEM)] * 4,
        out_specs=pl.BlockSpec(memory_space=pltpu.VMEM),
        compiler_params=pltpu.CompilerParams(vmem_limit_bytes=4 * 1024 * 1024),
        name="route_rows",
        cost_estimate=pl.CostEstimate(
            flops=2 * EXPERTS * rows * width, bytes_accessed=1 << 19, transcendentals=rows
        ),
    )(hidden_rows, parent_beam.reshape(1, rows), norm_gain.reshape(1, width), route_ids.T)


def shards(
    hidden_rows,
    parent_beam,
    norm_gain,
    route_ids,
    route_weight,
    expert_weight,
    learn_tokens,
    learn_live,
    cotangent,
    master,
    first_moment,
    second_moment,
):
    hid_local = master.shape[2]
    own_rows = master.shape[0]
    wide = 2 * hid_local
    n_y, n_z = lax.axis_size("y"), lax.axis_size("z")

    eighth = learn_tokens.shape[0] // 8
    tall_tokens = 8 * eighth
    core = lax.axis_index("core")

    def own_first(block):
        block = block.reshape(2, 2, 2, eighth, block.shape[1])
        for place, axis in enumerate(("core", "xl", "xh")):
            block = jnp.where(lax.axis_index(axis) == 1, jnp.flip(block, place), block)
        return block.reshape(tall_tokens, block.shape[4])

    rows_dev, width = hidden_rows.shape
    flat_ids = route_ids.reshape(rows_dev * TOP)
    onehot = (flat_ids[:, None] == jnp.arange(EXPERTS, dtype=jnp.int32)[None, :]).astype(jnp.int32)
    earlier = jnp.cumsum(onehot, axis=0) - onehot
    position = jnp.sum(earlier * onehot, axis=1)
    slot_index = flat_ids * CAP + position
    slot_table = (
        slot_index[:, None] == jnp.arange(EXPERTS * CAP, dtype=jnp.int32)[None, :]
    ).astype(jnp.float32)
    span = width // 2
    outgoing = route_rows(hidden_rows, parent_beam, norm_gain, route_ids)
    features = width // n_y
    chunks = span // features
    tokens_part = lax.dynamic_slice_in_dim(
        learn_tokens, (core * 4 + lax.axis_index(ALONG_X)) * eighth, eighth, 0
    )
    along_y = jnp.concatenate(
        [
            tokens_part.reshape(eighth, n_y, features).transpose(1, 0, 2),
            outgoing.reshape(n_y, n_z * chunks, features),
        ],
        axis=1,
    )
    along_y = lax.all_to_all(along_y, "y", split_axis=0, concat_axis=0, tiled=True)
    local_weight = expert_weight.reshape(width, wide)
    along_y, local_weight = lax.optimization_barrier((along_y, local_weight))
    own_slice = stack_rows(with_neighbours(along_y[:, :eighth]))
    other_slice = lax.ppermute(own_slice, "core", SWAP)
    token_slice = jnp.concatenate([own_slice, other_slice], axis=1).reshape(n_y * tall_tokens, features)
    lanes = 2 * wide
    tall = n_z * chunks
    routed = along_y[:, eighth:].reshape(n_y, n_z, chunks, features).transpose(1, 0, 2, 3)
    routed = jnp.pad(
        routed.reshape(n_z, n_y * chunks, features), ((0, 0), (0, 0), (0, lanes - features))
    )
    low = master.astype(jnp.bfloat16).reshape(own_rows, wide)
    low = jnp.concatenate(
        [low[:tall], jnp.pad(low[tall:], ((0, 2 * tall - own_rows), (0, 0)))], axis=1
    )
    along_z = jnp.concatenate([routed, jnp.broadcast_to(low[None], (n_z,) + low.shape)], axis=1)
    along_z = lax.all_to_all(along_z, "z", split_axis=0, concat_axis=0, tiled=True)
    arrived = along_z[:, : n_y * chunks, :features].reshape(n_z * n_y, span)
    weights = jnp.concatenate(
        [
            along_z[:, n_y * chunks :, :wide],
            along_z[:, n_y * chunks : n_y * chunks + own_rows - tall, wide:],
        ],
        axis=1,
    ).reshape(n_z * own_rows, wide)

    partial_pre = to_half(
        jnp.dot(token_slice, weights, preferred_element_type=jnp.float32), pre_scale
    )
    partial_pre = partial_pre.reshape(n_y, tall_tokens, wide)
    pre_parts = lax.all_to_all(partial_pre, "y", split_axis=0, concat_axis=0, tiled=True)
    pieces = with_neighbours(arrived[None])
    projected = jnp.sum(pre_parts.astype(jnp.float32), axis=0) * (1.0 / pre_scale)
    gate_pre = projected[:, :hid_local]
    up_pre = projected[:, hid_local:]
    sigmoid_gate = jax.nn.sigmoid(gate_pre)
    upstream = own_first(cotangent).astype(jnp.float32) * own_first(
        learn_live.astype(jnp.float32)[:, None]
    )
    slope = sigmoid_gate * (1.0 + gate_pre * (1.0 - sigmoid_gate))
    grad_pre = jnp.concatenate(
        [upstream * up_pre * slope, upstream * gate_pre * sigmoid_gate], axis=1
    ).astype(jnp.bfloat16)

    grad_all = gather_by_exchange(grad_pre, "y").reshape(token_slice.shape[0], wide)
    pieces = stack_rows(pieces)[0]
    other_pieces = lax.ppermute(pieces, "core", SWAP)
    projected_rows = jnp.dot(
        jnp.where(core == 0, pieces, other_pieces),
        local_weight[:span],
        preferred_element_type=jnp.float32,
    ) + jnp.dot(
        jnp.where(core == 0, other_pieces, pieces),
        local_weight[span:],
        preferred_element_type=jnp.float32,
    )
    gate_rows = projected_rows[:, :hid_local]
    activated_rows = (
        gate_rows * jax.nn.sigmoid(gate_rows) * projected_rows[:, hid_local:]
    ).astype(jnp.bfloat16)
    activated_rows = activated_rows.reshape(2, 2, n_z, n_y, hid_local)
    for place, axis in enumerate(ALONG_X):
        activated_rows = jnp.where(
            lax.axis_index(axis) == 1, jnp.flip(activated_rows, place), activated_rows
        )
    activated_rows = activated_rows.transpose(2, 3, 1, 0, 4).reshape(n_z, n_y * 2, wide)
    grad_all, activated_rows = lax.optimization_barrier((grad_all, activated_rows))
    partial = lax.dot_general(
        token_slice, grad_all, (((0,), (0,)), ((), ())), preferred_element_type=jnp.float32
    ).astype(jnp.bfloat16)
    along_z = jnp.concatenate([partial.reshape(n_z, own_rows, wide), activated_rows], axis=1)
    along_z = lax.all_to_all(along_z, "z", split_axis=0, concat_axis=0, tiled=True)
    gradient = jnp.sum(along_z[:, :own_rows].astype(jnp.float32), axis=0).reshape(master.shape)
    returned = along_z[:, own_rows:].reshape(n_z, n_y, 2, wide).transpose(1, 0, 2, 3)
    new_first = beta_one * first_moment + (1.0 - beta_one) * gradient
    new_second = beta_two * second_moment + (1.0 - beta_two) * gradient * gradient
    correct_one = 1.0 - beta_one**adam_step
    correct_two = 1.0 - beta_two**adam_step
    update = new_first / correct_one / (jnp.sqrt(new_second / correct_two) + epsilon)
    new_master = master - learn_rate * (update + decay_rate * master)
    fresh_rows = new_master.astype(jnp.bfloat16).reshape(own_rows, wide)

    along_y = jnp.concatenate(
        [
            jnp.broadcast_to(fresh_rows[None], (n_y,) + fresh_rows.shape),
            returned.reshape(n_y, n_z * 2, wide),
        ],
        axis=1,
    )
    along_y = lax.all_to_all(along_y, "y", split_axis=0, concat_axis=0, tiled=True)
    fresh_rows = to_half(along_y[:, :own_rows].reshape(n_y * own_rows, wide), fresh_scale)
    returned = along_y[:, own_rows:]
    fresh = lax.all_gather(fresh_rows, "z", axis=0, tiled=True)
    fresh = from_half(fresh, fresh_scale).reshape(n_z, n_y, own_rows, wide)
    fresh = fresh.transpose(1, 0, 2, 3).reshape(n_y * n_z * own_rows, wide)
    fresh = lax.optimization_barrier(fresh).reshape(n_y * n_z * own_rows, 2, hid_local)
    back_slots = returned.reshape(EXPERTS, 2, 2, hid_local).transpose(0, 2, 1, 3)
    back_slots = back_slots.reshape(EXPERTS * CAP, hid_local)
    picked = jnp.dot(
        slot_table.astype(jnp.bfloat16), back_slots, preferred_element_type=jnp.float32
    )
    rolled = (
        (picked * route_weight.reshape(rows_dev * TOP, 1))
        .astype(jnp.bfloat16)
        .reshape(rows_dev, TOP, hid_local)
    )
    return (rolled, new_master, new_first, new_second, fresh)


def solution(mesh):
    fine = Mesh(mesh.devices.reshape(2, 2, 8, 8, 2), ("xl", "core", "y", "z", "xh"))
    placed = (
        P(ROW, None),
        P(ROW),
        P(),
        P(ROW, None),
        P(ROW, None),
        P(ROW, None, None, COLUMN),
        P(ROW, None),
        P(ROW),
        P(ROW, COLUMN),
        P(ROW, None, COLUMN),
        P(ROW, None, COLUMN),
        P(ROW, None, COLUMN),
    )
    return jax.shard_map(
        shards,
        mesh=fine,
        in_specs=placed,
        out_specs=(
            P(ROW, None, COLUMN),
            P(ROW, None, COLUMN),
            P(ROW, None, COLUMN),
            P(ROW, None, COLUMN),
            P(None, None, COLUMN),
        ),
        check_vma=False,
    )
```

```python
import jax
import jax.numpy as jnp
from jax import lax
from jax.experimental import pallas as pl
from jax.experimental.pallas import tpu as pltpu
from jax.sharding import Mesh, PartitionSpec as P

EXPERTS = 64
TOP = 8
BEAMS = 4
CAP = 4

beta_one = 0.9
beta_two = 0.95
learn_rate = 0.01
decay_rate = 0.1
epsilon = 1e-08
norm_epsilon = 1e-06
adam_step = 10.0

ROW = ("y", "z")
COLUMN = ("xl", "core", "xh")
ALONG_X = ("xl", "xh")
SWAP = [(0, 1), (1, 0)]
pre_scale = 2.0**7
fresh_scale = 2.0**16


def to_half(values, scale):
    return (values.astype(jnp.float32) * scale).astype(jnp.float16)


def from_half(values, scale):
    return (values.astype(jnp.float32) * (1.0 / scale)).astype(jnp.bfloat16)


def gather_by_exchange(block, axis):
    count = lax.axis_size(axis)
    return lax.all_to_all(
        jnp.broadcast_to(block[None], (count,) + block.shape), axis, 0, 0, tiled=True
    )


def stack_kernel(*refs):
    blocks, stacked = refs[:-1], refs[-1]
    rows = blocks[0].shape[1]
    for k, block in enumerate(blocks):
        stacked[:, k * rows : (k + 1) * rows] = block[...]


def stack_rows(blocks):
    outer, rows, columns = blocks[0].shape
    count = len(blocks)
    return pl.pallas_call(
        stack_kernel,
        out_shape=jax.ShapeDtypeStruct((outer, count * rows, columns), blocks[0].dtype),
        in_specs=[pl.BlockSpec(memory_space=pltpu.VMEM)] * count,
        out_specs=pl.BlockSpec(memory_space=pltpu.VMEM),
        compiler_params=pltpu.CompilerParams(vmem_limit_bytes=4 * 1024 * 1024),
        name="stack_rows",
        cost_estimate=pl.CostEstimate(
            flops=0, bytes_accessed=4 * count * outer * rows * columns, transcendentals=0
        ),
    )(*blocks)


def with_neighbours(block):
    return [block] + [
        lax.ppermute(block, ALONG_X, [(i, i ^ k) for i in range(4)]) for k in range(1, 4)
    ]


def route_kernel(hidden_ref, gain_ref, ids_ref, out_ref):
    rows, width = hidden_ref.shape
    core = lax.axis_index("core")
    slot = (lax.axis_index("xl") * 2 + lax.axis_index("xh")).astype(jnp.float32)
    hidden = hidden_ref[...].astype(jnp.float32)
    mean_square = jnp.mean(hidden * hidden, axis=1, keepdims=True)
    normed = (hidden * lax.rsqrt(mean_square + norm_epsilon) * gain_ref[...]).astype(jnp.bfloat16)
    ids = ids_ref[...]
    expert = lax.broadcasted_iota(jnp.int32, (EXPERTS, rows), 0)
    named = jnp.zeros((EXPERTS, rows), jnp.float32)
    for k in range(TOP):
        named = named + (expert == ids[k : k + 1, :]).astype(jnp.float32)
    first = lax.broadcasted_iota(jnp.int32, (rows, rows), 0)
    second = lax.broadcasted_iota(jnp.int32, (rows, rows), 1)
    earlier = jnp.dot(
        named, (first < second).astype(jnp.float32), preferred_element_type=jnp.float32
    )
    sends = jnp.where(earlier == slot, named, 0.0)
    parent = second - (second & (BEAMS - 1)) + ids[TOP : TOP + 1, :]
    source = (first == parent).astype(jnp.float32)
    table = lax.dot_general(
        sends, source, (((1,), (1,)), ((), ())), preferred_element_type=jnp.float32
    ).astype(jnp.bfloat16)

    @pl.when(core == 0)
    def _():
        out_ref[...] = jnp.dot(
            table, normed[:, : width // 2], preferred_element_type=jnp.float32
        ).astype(jnp.bfloat16)

    @pl.when(core != 0)
    def _():
        out_ref[...] = jnp.dot(
            table, normed[:, width // 2 :], preferred_element_type=jnp.float32
        ).astype(jnp.bfloat16)


def route_rows(hidden_rows, parent_beam, norm_gain, route_ids):
    rows, width = hidden_rows.shape
    return pl.pallas_call(
        route_kernel,
        out_shape=jax.ShapeDtypeStruct((EXPERTS, width // 2), jnp.bfloat16),
        in_specs=[pl.BlockSpec(memory_space=pltpu.VMEM)] * 3,
        out_specs=pl.BlockSpec(memory_space=pltpu.VMEM),
        compiler_params=pltpu.CompilerParams(vmem_limit_bytes=4 * 1024 * 1024),
        name="route_rows",
        cost_estimate=pl.CostEstimate(
            flops=2 * EXPERTS * rows * width, bytes_accessed=1 << 19, transcendentals=rows
        ),
    )(
        hidden_rows,
        norm_gain.reshape(1, width),
        jnp.concatenate([route_ids.T, parent_beam.reshape(1, rows)], axis=0),
    )


def shards(
    hidden_rows,
    parent_beam,
    norm_gain,
    route_ids,
    route_weight,
    expert_weight,
    learn_tokens,
    learn_live,
    cotangent,
    master,
    first_moment,
    second_moment,
):
    hid_local = master.shape[2]
    own_rows = master.shape[0]
    wide = 2 * hid_local
    n_y, n_z = lax.axis_size("y"), lax.axis_size("z")

    eighth = learn_tokens.shape[0] // 8
    tall_tokens = 8 * eighth
    core = lax.axis_index("core")

    def own_first(block):
        block = block.reshape(2, 2, 2, eighth, block.shape[1])
        for place, axis in enumerate(("core", "xl", "xh")):
            block = jnp.where(lax.axis_index(axis) == 1, jnp.flip(block, place), block)
        return block.reshape(tall_tokens, block.shape[4])

    rows_dev, width = hidden_rows.shape
    flat_ids = route_ids.reshape(rows_dev * TOP)
    onehot = (flat_ids[:, None] == jnp.arange(EXPERTS, dtype=jnp.int32)[None, :]).astype(jnp.int32)
    earlier = jnp.cumsum(onehot, axis=0) - onehot
    position = jnp.sum(earlier * onehot, axis=1)
    slot_index = flat_ids * CAP + position
    slot_table = (
        slot_index[:, None] == jnp.arange(EXPERTS * CAP, dtype=jnp.int32)[None, :]
    ).astype(jnp.float32)
    span = width // 2
    outgoing = route_rows(hidden_rows, parent_beam, norm_gain, route_ids)
    features = width // n_y
    chunks = span // features
    tokens_part = lax.dynamic_slice_in_dim(
        learn_tokens, (core * 4 + lax.axis_index(ALONG_X)) * eighth, eighth, 0
    )
    along_y = jnp.concatenate(
        [
            tokens_part.reshape(eighth, n_y, features).transpose(1, 0, 2),
            outgoing.reshape(n_y, n_z * chunks, features),
        ],
        axis=1,
    )
    along_y = lax.all_to_all(along_y, "y", split_axis=0, concat_axis=0, tiled=True)
    local_weight = expert_weight.reshape(width, wide)
    along_y, local_weight = lax.optimization_barrier((along_y, local_weight))
    own_slice = stack_rows(with_neighbours(along_y[:, :eighth]))
    other_slice = lax.ppermute(own_slice, "core", SWAP)
    token_slice = jnp.concatenate([own_slice, other_slice], axis=1).reshape(n_y * tall_tokens, features)
    lanes = 2 * wide
    tall = n_z * chunks
    routed = along_y[:, eighth:].reshape(n_y, n_z, chunks, features).transpose(1, 0, 2, 3)
    routed = jnp.pad(
        routed.reshape(n_z, n_y * chunks, features), ((0, 0), (0, 0), (0, lanes - features))
    )
    low = master.astype(jnp.bfloat16).reshape(own_rows, wide)
    low = jnp.concatenate(
        [low[:tall], jnp.pad(low[tall:], ((0, 2 * tall - own_rows), (0, 0)))], axis=1
    )
    along_z = jnp.concatenate([routed, jnp.broadcast_to(low[None], (n_z,) + low.shape)], axis=1)
    along_z = lax.all_to_all(along_z, "z", split_axis=0, concat_axis=0, tiled=True)
    arrived = along_z[:, : n_y * chunks, :features].reshape(n_z * n_y, span)
    weights = jnp.concatenate(
        [
            along_z[:, n_y * chunks :, :wide],
            along_z[:, n_y * chunks : n_y * chunks + own_rows - tall, wide:],
        ],
        axis=1,
    ).reshape(n_z * own_rows, wide)

    partial_pre = to_half(
        jnp.dot(token_slice, weights, preferred_element_type=jnp.float32), pre_scale
    )
    partial_pre = partial_pre.reshape(n_y, tall_tokens, wide)
    pre_parts = lax.all_to_all(partial_pre, "y", split_axis=0, concat_axis=0, tiled=True)
    pieces = with_neighbours(arrived[None])
    projected = jnp.sum(pre_parts.astype(jnp.float32), axis=0) * (1.0 / pre_scale)
    gate_pre = projected[:, :hid_local]
    up_pre = projected[:, hid_local:]
    sigmoid_gate = jax.nn.sigmoid(gate_pre)
    upstream = own_first(cotangent).astype(jnp.float32) * own_first(
        learn_live.astype(jnp.float32)[:, None]
    )
    slope = sigmoid_gate * (1.0 + gate_pre * (1.0 - sigmoid_gate))
    grad_pre = jnp.concatenate(
        [upstream * up_pre * slope, upstream * gate_pre * sigmoid_gate], axis=1
    ).astype(jnp.bfloat16)

    grad_all = gather_by_exchange(grad_pre, "y").reshape(token_slice.shape[0], wide)
    pieces = stack_rows(pieces)[0]
    other_pieces = lax.ppermute(pieces, "core", SWAP)
    projected_rows = jnp.dot(
        jnp.where(core == 0, pieces, other_pieces),
        local_weight[:span],
        preferred_element_type=jnp.float32,
    ) + jnp.dot(
        jnp.where(core == 0, other_pieces, pieces),
        local_weight[span:],
        preferred_element_type=jnp.float32,
    )
    gate_rows = projected_rows[:, :hid_local]
    activated_rows = (
        gate_rows * jax.nn.sigmoid(gate_rows) * projected_rows[:, hid_local:]
    ).astype(jnp.bfloat16)
    activated_rows = activated_rows.reshape(2, 2, n_z, n_y, hid_local)
    for place, axis in enumerate(ALONG_X):
        activated_rows = jnp.where(
            lax.axis_index(axis) == 1, jnp.flip(activated_rows, place), activated_rows
        )
    activated_rows = activated_rows.transpose(2, 3, 1, 0, 4).reshape(n_z, n_y * 2, wide)
    grad_all, activated_rows = lax.optimization_barrier((grad_all, activated_rows))
    partial = lax.dot_general(
        token_slice, grad_all, (((0,), (0,)), ((), ())), preferred_element_type=jnp.float32
    ).astype(jnp.bfloat16)
    along_z = jnp.concatenate([partial.reshape(n_z, own_rows, wide), activated_rows], axis=1)
    along_z = lax.all_to_all(along_z, "z", split_axis=0, concat_axis=0, tiled=True)
    gradient = jnp.sum(along_z[:, :own_rows].astype(jnp.float32), axis=0).reshape(master.shape)
    returned = along_z[:, own_rows:].reshape(n_z, n_y, 2, wide).transpose(1, 0, 2, 3)
    new_first = beta_one * first_moment + (1.0 - beta_one) * gradient
    new_second = beta_two * second_moment + (1.0 - beta_two) * gradient * gradient
    correct_one = 1.0 - beta_one**adam_step
    correct_two = 1.0 - beta_two**adam_step
    update = new_first / correct_one / (jnp.sqrt(new_second / correct_two) + epsilon)
    new_master = master - learn_rate * (update + decay_rate * master)
    fresh_rows = new_master.astype(jnp.bfloat16).reshape(own_rows, wide)

    along_y = jnp.concatenate(
        [
            jnp.broadcast_to(fresh_rows[None], (n_y,) + fresh_rows.shape),
            returned.reshape(n_y, n_z * 2, wide),
        ],
        axis=1,
    )
    along_y = lax.all_to_all(along_y, "y", split_axis=0, concat_axis=0, tiled=True)
    fresh_rows = to_half(along_y[:, :own_rows].reshape(n_y * own_rows, wide), fresh_scale)
    returned = along_y[:, own_rows:]
    fresh = lax.all_gather(fresh_rows, "z", axis=0, tiled=True)
    fresh = from_half(fresh, fresh_scale).reshape(n_z, n_y, own_rows, wide)
    fresh = fresh.transpose(1, 0, 2, 3).reshape(n_y * n_z * own_rows, wide)
    fresh = lax.optimization_barrier(fresh).reshape(n_y * n_z * own_rows, 2, hid_local)
    back_slots = returned.reshape(EXPERTS, 2, 2, hid_local).transpose(0, 2, 1, 3)
    back_slots = back_slots.reshape(EXPERTS * CAP, hid_local)
    picked = jnp.dot(
        slot_table.astype(jnp.bfloat16), back_slots, preferred_element_type=jnp.float32
    )
    rolled = (
        (picked * route_weight.reshape(rows_dev * TOP, 1))
        .astype(jnp.bfloat16)
        .reshape(rows_dev, TOP, hid_local)
    )
    return (rolled, new_master, new_first, new_second, fresh)


def solution(mesh):
    fine = Mesh(mesh.devices.reshape(2, 2, 8, 8, 2), ("xl", "core", "y", "z", "xh"))
    placed = (
        P(ROW, None),
        P(ROW),
        P(),
        P(ROW, None),
        P(ROW, None),
        P(ROW, None, None, COLUMN),
        P(ROW, None),
        P(ROW),
        P(ROW, COLUMN),
        P(ROW, None, COLUMN),
        P(ROW, None, COLUMN),
        P(ROW, None, COLUMN),
    )
    return jax.shard_map(
        shards,
        mesh=fine,
        in_specs=placed,
        out_specs=(
            P(ROW, None, COLUMN),
            P(ROW, None, COLUMN),
            P(ROW, None, COLUMN),
            P(ROW, None, COLUMN),
            P(None, None, COLUMN),
        ),
        check_vma=False,
    )
```
